512 devices in a mesh: seq: 64 (over z, y_hi, core), tp: 8 (over x, y_lo).
Axes of the slice: x: 4, y: 4 (y_hi: 2, y_lo: 2; y = y_hi * 2 + y_lo), z: 16, core: 2. Of those that a mesh axis runs over, the one named last changes fastest.
Arguments:
- q_proj: bfloat16 [8192, 8192], P('seq', 'tp'), may hold values from -6 to 6
- k_proj: bfloat16 [8192, 8192], P('seq', 'tp'), may hold values from -6 to 6
- v_proj: bfloat16 [8192, 8192], P('seq', 'tp'), may hold values from -6 to 6
- grad_out: bfloat16 [8192, 8192], P('seq', 'tp'), may hold values from -6 to 6
- w_first: float32 [32, 64], replicated, may hold values from -2 to 2
- w_second: float32 [64, 8192], P(None, 'tp'), may hold values from -0.75 to 0.75
- decay_rate: float32 [8192], P('tp'), may hold values from 0.02 to 256
- skip_gain: float32 [8192], P('tp'), may hold values from 0.5 to 1.5
Outputs:
- grad_q: bfloat16 [8192, 8192], P('seq', 'tp')
- grad_k: bfloat16 [8192, 8192], P('seq', 'tp')
- grad_v: bfloat16 [8192, 8192], P('seq', 'tp')
- grad_first: float32 [32, 64], replicated
- grad_second: float32 [64, 8192], P(None, 'tp')
- grad_decay: float32 [8192], P('tp')
- grad_skip: float32 [8192], P('tp')
The draws below stay inside these ranges and needn't reach their ends.
All inputs are finite; a program needn't handle non-finite values.
Results may differ from the reference program's by a relative error of at most 0.0058.
Values may be sent and summed in bfloat16 or wider, within the bound.
A program may use at most 64 MiB of HBM per device.

```python
import math
import jax
import jax.numpy as jnp
from jax import lax

D = 8192
F = 64
E = 32
SEQ = 8192


def block_levels(own_key, shape, split, smallest, largest):
    def one(axis_at, parts):
        heights = jax.random.uniform(jax.random.fold_in(jax.random.fold_in(own_key, 6), axis_at), (parts,), jnp.float32, smallest / len(split), largest / len(split))
        return jnp.repeat(jnp.exp(heights), shape[axis_at] // parts).reshape((-1,) + (1,) * (len(shape) - axis_at - 1))

    level = one(*split[0])
    for cut in split[1:]:
        level = level * one(*cut)
    return level


def noise(rng, dims, scale, most, pieces=(), held_as=jnp.bfloat16):
    level = block_levels(rng, dims, pieces, -0.22, 0.18) if pieces else 1.0
    values = jax.random.normal(rng, dims, jnp.float32) * scale * level
    return jnp.minimum(jnp.maximum(values, -most), most).astype(held_as)


def setup_inputs(seed: int = 0) -> dict:
    streams_of = jax.random.split(jax.random.key(seed), 9)
    q_proj = noise(streams_of[0], (SEQ, D), 1.0, 6.0, ((0, 64), (1, 8)))
    k_proj = noise(streams_of[1], (SEQ, D), 1.0, 6.0, ((0, 64), (1, 8)))
    v_proj = noise(streams_of[2], (SEQ, D), 1.0, 6.0, ((0, 64), (1, 8)))
    grad_out = noise(streams_of[3], (SEQ, D), 1.0, 6.0, ((0, 64), (1, 8)))
    w_first = noise(streams_of[4], (E, F), (E // 4) ** -0.5, 2.0, (), jnp.float32)
    w_second = noise(streams_of[5], (F, D), F ** -0.5, 0.75, ((1, 8),), jnp.float32)
    decay_rate = jnp.clip(jnp.exp(math.log(256.0) - 9.4572 * jax.random.uniform(streams_of[6], (D,), jnp.float32) ** block_levels(streams_of[6], (D,), ((0, 8),), -0.2, 0.2)), 0.02, 256.0)
    skip_gain = jnp.clip(0.5 + 1.0 * jax.random.uniform(streams_of[7], (D,), jnp.float32) ** block_levels(streams_of[7], (D,), ((0, 8),), -0.2, 0.2), 0.5, 1.5)
    return {"q_proj": q_proj, "k_proj": k_proj, "v_proj": v_proj, "grad_out": grad_out, "w_first": w_first, "w_second": w_second, "decay_rate": decay_rate, "skip_gain": skip_gain}


HIGH = lax.Precision.HIGHEST


def positional_table(length, band_count):
    positions = jnp.arange(length, dtype=jnp.int32)
    band_index = jnp.arange(band_count, dtype=jnp.int32)
    frequency = 3 * (band_index + 1) * (band_index + 1) + band_index
    phase_index = (positions[:, None] * frequency[None, :]) % length
    angles = phase_index.astype(jnp.float32) * (2.0 * math.pi / length)
    return jnp.concatenate([jnp.sin(angles), jnp.cos(angles)], axis=1)


def reference(q_proj, k_proj, v_proj, grad_out, w_first, w_second, decay_rate, skip_gain):
    length = SEQ
    scale_seq = length ** -0.5
    padded_len = 2 * length
    positional = positional_table(length, E // 2)
    sine_input = jnp.dot(positional, w_first, precision=HIGH, preferred_element_type=jnp.float32)
    hidden = jnp.sin(sine_input)
    gated_in = (k_proj.astype(jnp.float32) * v_proj.astype(jnp.float32)).astype(jnp.bfloat16)
    gated_grad = (grad_out.astype(jnp.float32) * q_proj.astype(jnp.float32)).astype(jnp.bfloat16)
    block_width = math.gcd(D, 512)
    block_count = D // block_width
    fraction = jnp.arange(length).astype(jnp.float32) / length

    def one_block(grad_hidden, block_index):
        block_start = (block_index * block_width).astype(jnp.int32)
        gated_full = lax.dynamic_slice_in_dim(gated_in, block_start, block_width, 1).astype(jnp.float32)
        grad_full = lax.dynamic_slice_in_dim(gated_grad, block_start, block_width, 1).astype(jnp.float32)
        w_block = lax.dynamic_slice_in_dim(w_second, block_start, block_width, 1)
        decay_block = lax.dynamic_slice_in_dim(decay_rate, block_start, block_width, 0)
        skip_block = lax.dynamic_slice_in_dim(skip_gain, block_start, block_width, 0)
        raw_filter = jnp.dot(hidden, w_block, precision=HIGH, preferred_element_type=jnp.float32)
        envelope = jnp.exp(-decay_block[None, :] * fraction[:, None])
        long_filter = raw_filter * envelope * scale_seq
        spectrum_filter = jnp.fft.rfft(long_filter, n=padded_len, axis=0)
        spectrum_in = jnp.fft.rfft(gated_full, n=padded_len, axis=0)
        spectrum_grad = jnp.fft.rfft(grad_full, n=padded_len, axis=0)
        convolved = jnp.fft.irfft(spectrum_filter * spectrum_in, n=padded_len, axis=0)[:length]
        convolved = convolved + skip_block[None, :] * gated_full
        grad_gated = jnp.fft.irfft(jnp.conj(spectrum_filter) * spectrum_grad, n=padded_len, axis=0)[:length]
        grad_gated = grad_gated + skip_block[None, :] * grad_full
        grad_filter = jnp.fft.irfft(jnp.conj(spectrum_in) * spectrum_grad, n=padded_len, axis=0)[:length]
        grad_raw = grad_filter * envelope * scale_seq
        grad_skip = jnp.sum(grad_full * gated_full, axis=0) * scale_seq
        grad_decay = -jnp.sum(grad_raw * raw_filter * fraction[:, None], axis=0) * scale_seq
        grad_second = jnp.dot(hidden.T, grad_raw, precision=HIGH, preferred_element_type=jnp.float32) * scale_seq
        grad_hidden = grad_hidden + jnp.dot(grad_raw, w_block.T, precision=HIGH, preferred_element_type=jnp.float32)
        return grad_hidden, (convolved.astype(jnp.bfloat16), grad_gated.astype(jnp.bfloat16), grad_skip, grad_decay, grad_second)

    grad_hidden, stacked = lax.scan(one_block, jnp.zeros((length, F), jnp.float32), jnp.arange(block_count))
    convolved, grad_gated, grad_skip, grad_decay, grad_second = stacked
    convolved = jnp.transpose(convolved, (1, 0, 2)).reshape(length, D)
    grad_gated = jnp.transpose(grad_gated, (1, 0, 2)).reshape(length, D).astype(jnp.float32)
    grad_second = jnp.transpose(grad_second, (1, 0, 2)).reshape(F, D)
    grad_skip = grad_skip.reshape(D)
    grad_decay = grad_decay.reshape(D)
    grad_q = (grad_out.astype(jnp.float32) * convolved.astype(jnp.float32)).astype(jnp.bfloat16)
    grad_k = (grad_gated * v_proj.astype(jnp.float32)).astype(jnp.bfloat16)
    grad_v = (grad_gated * k_proj.astype(jnp.float32)).astype(jnp.bfloat16)
    grad_first = jnp.dot(positional.T, grad_hidden * jnp.cos(sine_input), precision=HIGH, preferred_element_type=jnp.float32) * scale_seq
    return (grad_q, grad_k, grad_v, grad_first, grad_second, grad_decay, grad_skip)
```

```python
import functools
import math

import jax
import jax.numpy as jnp
import numpy as np
from jax import lax
from jax.experimental import pallas as pl
from jax.experimental.pallas import tpu as pltpu
from jax.sharding import PartitionSpec as P

MESH = pl.DeviceIdType.MESH
F32 = jnp.float32
BF16 = jnp.bfloat16
J = 64
B = 128
C = 16
L = J * B
GROUP = 4
SEQ = 64
TP = 8
DEPTH = 16
PLANE = 4


def split_np(values):
    high = values.astype(np.float32).astype(jnp.bfloat16)
    low = (values - high.astype(np.float64)).astype(np.float32).astype(jnp.bfloat16)
    return high, low


def make_tables():
    turn = 2.0 * math.pi
    k1 = np.arange(J)[:, None] + 0.25
    first = turn * k1 * np.arange(J)[None, :] / J
    f1_high, f1_low = split_np(np.concatenate([np.cos(first), -np.sin(first)], axis=0))
    twiddle = turn * k1 * np.arange(B)[None, :] / L
    second = turn * (np.arange(B)[:, None] * np.arange(B)[None, :] % B) / B
    cos, sin = np.cos(second), np.sin(second)
    f2_high, f2_low = split_np(np.block([[cos, -sin], [sin, cos]]))
    i1_high, i1_low = split_np(np.block([[cos, sin], [-sin, cos]]))
    i2_high, i2_low = split_np(np.concatenate([np.cos(first.T), -np.sin(first.T)], axis=1) / L)
    band = np.arange(16)
    freq = 3 * (band + 1) ** 2 + band
    inner = turn * (freq[:, None] * np.arange(B)[None, :] % L) / L
    p_high, p_low = split_np(np.concatenate([np.sin(inner), np.cos(inner)], axis=0))
    outer = turn * (np.arange(J)[:, None] * freq[None, :] % J) / J
    pos_t = np.zeros((3 * B, B), np.float32).astype(jnp.bfloat16)
    for at, part in enumerate((p_high, p_high, p_low)):
        pos_t[at * B : (at + 1) * B, :32] = part.T
    turn_cos = np.tile(np.concatenate([np.cos(outer), np.cos(outer)], axis=1), (1, 4))
    turn_sin = np.tile(np.concatenate([-np.sin(outer), np.sin(outer)], axis=1), (1, 4))
    return (
        np.concatenate([f1_high, f1_low], axis=1),
        np.concatenate([f1_high, f1_low, f1_high], axis=1),
        np.concatenate([f2_high, f2_high, f2_low], axis=0),
        np.concatenate([i1_high, i1_high, i1_low], axis=0),
        np.concatenate([i2_high, i2_low, i2_high], axis=1),
        np.cos(twiddle).astype(np.float32),
        np.sin(twiddle).astype(np.float32),
        np.concatenate([p_high, p_low, p_high, p_low], axis=0),
        pos_t,
        turn_cos.astype(np.float32),
        turn_sin.astype(np.float32),
    )


def dot(left, right):
    return jnp.dot(left, right, preferred_element_type=F32)


def split(values):
    high = values.astype(BF16)
    return high, (values - high.astype(F32)).astype(BF16)


def sin_cos(x):
    n = jnp.floor(x * (1.0 / math.pi) + 0.5)
    r = (x - n * 3.140625) - n * 9.6765358979e-4
    half = n * 0.5
    sign = 1.0 - 4.0 * (half - jnp.floor(half))
    s = r * r
    p = -1.0 / 39916800.0
    for factor in (1.0 / 362880.0, -1.0 / 5040.0, 1.0 / 120.0, -1.0 / 6.0):
        p = p * s + factor
    sine = (r + r * s * p) * sign
    q = 1.0 / 479001600.0
    for factor in (-1.0 / 3628800.0, 1.0 / 40320.0, -1.0 / 720.0, 1.0 / 24.0, -0.5, 1.0):
        q = q * s + factor
    return sine, q * sign


def kernel(
    q_ref, k_ref, v_ref, go_ref, w1_ref, w2_ref, decay_ref, skip_ref,
    f1x_ref, f1_ref, f2_ref, i1_ref, i2_ref, twc_ref, tws_ref, pb_ref, pt_ref, tc_ref, ts_ref,
    gq_ref, gk_ref, gv_ref, first_ref, second_ref, gdecay_ref, gskip_ref,
    send_x, send_g, in_x, in_g, back_x, back_g, conv_in, grad_in,
    params, stage, stage_x, raw_ref, env_ref, hid_hi, hid_lo, cos_ref, spec_h, spec_x, spec_g, wide,
    gather, rs_out, rs_in, plane_in, tp_in, fin,
    send_sem, x_sem, g_sem, cx_sem, cg_sem, z_sem, rz_sem, y_sem, ry_sem, t_sem, f_sem,
):
    me = lax.axis_index("seq")
    my_tp = lax.axis_index("tp")
    my_z, my_y = me // PLANE, me % PLANE
    scale = L**-0.5

    barrier = pltpu.get_barrier_semaphore()

    def greet(i, carry):
        pl.semaphore_signal(
            barrier, inc=1, device_id={"seq": (me + i) % SEQ}, device_id_type=MESH
        )
        return carry

    lax.fori_loop(1, SEQ, greet, 0)

    def greet_tp(i, carry):
        pl.semaphore_signal(
            barrier, inc=1, device_id={"tp": (my_tp + i) % TP}, device_id_type=MESH
        )
        return carry

    lax.fori_loop(1, TP, greet_tp, 0)

    def gate(left_ref, right_ref, out_ref):
        def step(at, carry):
            parts = []
            for half in range(2):
                lanes = pl.ds(pl.multiple_of(half * 512 + at * B, B), B)
                gated = left_ref[:, lanes].astype(F32) * right_ref[:, lanes].astype(F32)
                parts.append(jnp.transpose(gated).reshape(16, 8, B))
            out_ref[pl.ds(at * 16, 16)] = jnp.concatenate(parts, axis=1).astype(BF16)
            return carry

        lax.fori_loop(0, 4, step, 0)

    def exchange(out_ref, in_ref, recv_sem, send_at):
        def step(i, carry):
            for peer in ((me + i) % SEQ, (me + SEQ - i) % SEQ):
                pltpu.make_async_remote_copy(
                    src_ref=out_ref.at[peer],
                    dst_ref=in_ref.at[me],
                    send_sem=send_sem.at[send_at],
                    recv_sem=recv_sem,
                    device_id={"seq": peer},
                    device_id_type=MESH,
                ).start()
            return carry

        lax.fori_loop(1, SEQ // 2, step, 0)
        peer = (me + SEQ // 2) % SEQ
        pltpu.make_async_remote_copy(
            src_ref=out_ref.at[peer],
            dst_ref=in_ref.at[me],
            send_sem=send_sem.at[send_at],
            recv_sem=recv_sem,
            device_id={"seq": peer},
            device_id_type=MESH,
        ).start()
        in_ref[me] = out_ref[me]

    def wait_bytes(ref, count, sem):
        view = ref.at[pl.ds(0, count)]
        pltpu.make_async_copy(view, view, sem).wait()

    gate(k_ref, v_ref, send_x)
    pl.semaphore_wait(barrier, SEQ - 1 + TP - 1)
    exchange(send_x, in_x, x_sem, 0)
    gate(q_ref, go_ref, send_g)
    exchange(send_g, in_g, g_sem, 1)

    for half in range(2):
        lanes = pl.ds(pl.multiple_of(half * 512 + (me // 16) * B, B), B)
        rows = lax.broadcasted_iota(jnp.int32, (64, B), 0)
        tail = jnp.where(
            rows == 0,
            jnp.broadcast_to(decay_ref[:, lanes], (64, B)),
            jnp.where(rows == 1, jnp.broadcast_to(skip_ref[:, lanes], (64, B)), 0.0),
        )
        params[half] = jnp.transpose(jnp.concatenate([w2_ref[:, lanes], tail], axis=0))
    pick = pl.ds(pl.multiple_of((me % 16) * 8, 8), 8)
    mine = jnp.concatenate([params[0, pick, :], params[1, pick, :]], axis=0)
    lane = lax.broadcasted_iota(jnp.int32, (C, B), 1)
    weights = jnp.where(lane < 64, mine, 0.0)
    decay = jnp.sum(jnp.where(lane == 64, mine, 0.0), axis=1, keepdims=True)
    skip = jnp.sum(jnp.where(lane == 65, mine, 0.0), axis=1, keepdims=True)
    w_high = weights.astype(BF16).astype(F32)
    w_low = (weights - w_high).astype(BF16).astype(F32)
    w_pair = w_high + pltpu.roll(w_low, 64, 1)
    w_rows = jnp.concatenate([w_pair, w_pair], axis=1).astype(BF16)
    wide[...] = jnp.zeros((B, B), F32)
    for at, part in enumerate((w_high, w_low, w_high, w_low)):
        wide[at * C : (at + 1) * C, :] = part
    w_cols = jnp.transpose(wide[...])[:64, :64].astype(BF16)

    w_one = w1_ref[...]
    w_swap = jnp.concatenate([w_one[16:], w_one[:16]], axis=0)
    wide[:, :64] = jnp.concatenate([w_one] * 4, axis=0)
    turned = jnp.transpose(wide[...])[:64]
    wide[:, :64] = jnp.concatenate([w_swap] * 4, axis=0)
    turned_swap = jnp.transpose(wide[...])[:64]
    lane_b = lax.broadcasted_iota(jnp.int32, (GROUP * 64, B), 1)
    position = lax.broadcasted_iota(jnp.int32, (C, B), 1).astype(F32)

    def network(at, carry):
        pieces = []
        for i in range(GROUP):
            j = at * GROUP + i
            pieces.append(turned * tc_ref[pl.ds(j, 1), :] + turned_swap * ts_ref[pl.ds(j, 1), :])
        values = jnp.concatenate(pieces, axis=0)
        high = values.astype(BF16).astype(F32)
        left = jnp.where(lane_b < 64, high, values - high).astype(BF16)
        sine, cosine = sin_cos(dot(left, pb_ref[...]))
        rows = pl.ds(pl.multiple_of(at * GROUP * 64, GROUP * 64), GROUP * 64)
        cos_ref[rows, :] = cosine
        high, low = split(sine)
        hid_hi[rows, :] = high
        hid_lo[rows, :] = low
        for i in range(0, GROUP, 2):
            h = jnp.concatenate([high[i * 64 : (i + 1) * 64], high[(i + 1) * 64 : (i + 2) * 64]], axis=1)
            l = jnp.concatenate([low[i * 64 : (i + 1) * 64], low[(i + 1) * 64 : (i + 2) * 64]], axis=1)
            raw = dot(w_rows, jnp.concatenate([h, h, l, l], axis=0))
            for o in range(2):
                j = at * GROUP + i + o
                fraction = (position + (j * B).astype(F32)) * (1.0 / L)
                envelope = jnp.exp(-decay * fraction) * scale
                part = raw[:, o * B : (o + 1) * B]
                here = pl.ds(pl.multiple_of(j * C, C), C)
                raw_ref[here, :] = part
                env_ref[here, :] = envelope
                stage[here, :] = part * envelope
        return carry

    lax.fori_loop(0, J // GROUP, network, 0)

    def forward(from_ref, spec_ref, exact):
        def step(at, carry):
            cols = [from_ref[pl.ds(at * GROUP + i, J, stride=C), :] for i in range(GROUP)]
            data = jnp.concatenate(cols, axis=1)
            if exact:
                data = data.astype(BF16)
                mixed = dot(f1x_ref[...], jnp.concatenate([data, data], axis=0))
            else:
                high, low = split(data)
                mixed = dot(f1_ref[...], jnp.concatenate([high, high, low], axis=0))
            turned = []
            for i in range(GROUP):
                re, im = mixed[:J, i * B : (i + 1) * B], mixed[J:, i * B : (i + 1) * B]
                c, s = twc_ref[...], tws_ref[...]
                turned.append(jnp.concatenate([re * c + im * s, im * c - re * s], axis=1))
            high, low = split(jnp.concatenate(turned, axis=0))
            rows = pl.ds(pl.multiple_of(at * GROUP * J, GROUP * J), GROUP * J)
            spec_ref[rows, :] = dot(jnp.concatenate([high, low, high], axis=1), f2_ref[...])
            return carry

        lax.fori_loop(0, C // GROUP, step, 0)

    def inverse(left_ref, right_ref, conjugate):
        def step(at, carry):
            rows = pl.ds(pl.multiple_of(at * GROUP * J, GROUP * J), GROUP * J)
            a, b = left_ref[rows, :], right_ref[rows, :]
            ar, ai, br, bi = a[:, :B], a[:, B:], b[:, :B], b[:, B:]
            if conjugate:
                product = jnp.concatenate([ar * br + ai * bi, ar * bi - ai * br], axis=1)
            else:
                product = jnp.concatenate([ar * br - ai * bi, ar * bi + ai * br], axis=1)
            high, low = split(product)
            mixed = dot(jnp.concatenate([high, low, high], axis=1), i1_ref[...])
            turned = []
            for i in range(GROUP):
                re, im = mixed[i * J : (i + 1) * J, :B], mixed[i * J : (i + 1) * J, B:]
                c, s = twc_ref[...], tws_ref[...]
                turned.append(jnp.concatenate([re * c - im * s, re * s + im * c], axis=0))
            high, low = split(jnp.concatenate(turned, axis=1))
            result = dot(i2_ref[...], jnp.concatenate([high, high, low], axis=0))
            for i in range(GROUP):
                stage[pl.ds(at * GROUP + i, J, stride=C), :] = result[:, i * B : (i + 1) * B]
            return carry

        lax.fori_loop(0, C // GROUP, step, 0)

    def finish(in_ref, out_ref):
        def step(at, carry):
            blocks = pl.ds(at * 8, 8)
            rows = pl.ds(pl.multiple_of(at * 8 * C, 8 * C), 8 * C)
            values = stage[rows, :].reshape(8, C, B) + skip[None] * in_ref[blocks].astype(F32)
            out_ref[blocks] = values.astype(BF16)
            return carry

        lax.fori_loop(0, J // 8, step, 0)

    def widen(in_ref, to_ref):
        def step(at, carry):
            rows = pl.ds(pl.multiple_of(at * 8 * C, 8 * C), 8 * C)
            to_ref[rows, :] = in_ref[pl.ds(at * 8, 8)].astype(F32).reshape(8 * C, B)
            return carry

        lax.fori_loop(0, J // 8, step, 0)

    forward(stage, spec_h, False)
    wait_bytes(in_x, SEQ - 1, x_sem)
    widen(in_x, stage_x)
    forward(stage_x, spec_x, True)
    inverse(spec_h, spec_x, False)
    finish(in_x, back_x)
    exchange(back_x, conv_in, cx_sem, 2)

    wait_bytes(in_g, SEQ - 1, g_sem)
    widen(in_g, stage)
    forward(stage, spec_g, True)
    inverse(spec_h, spec_g, True)
    finish(in_g, back_g)
    exchange(back_g, grad_in, cg_sem, 3)

    inverse(spec_x, spec_g, True)

    def reduce_filter(at, carry):
        decay_sum, skip_sum, second, cos_sum, sin_sum = carry
        left, right, hid_rows = [], [], []
        for i in range(GROUP):
            j = at * GROUP + i
            here = pl.ds(pl.multiple_of(j * C, C), C)
            grad_raw = stage[here, :] * env_ref[here, :]
            fraction = (position + (j * B).astype(F32)) * (1.0 / L)
            decay_sum += grad_raw * raw_ref[here, :] * fraction
            skip_sum += in_x[j].astype(F32) * in_g[j].astype(F32)
            high, low = split(grad_raw)
            right.append(jnp.concatenate([high, high, low], axis=1))
            rows = pl.ds(pl.multiple_of(j * 64, 64), 64)
            h = hid_hi[rows, :]
            hid_rows.append(jnp.concatenate([h, hid_lo[rows, :], h], axis=1))
            left.append(dot(w_cols, jnp.concatenate([high, high, low, low], axis=0)))
        second += lax.dot_general(
            jnp.concatenate(hid_rows, axis=1),
            jnp.concatenate(right, axis=1),
            (((1,), (1,)), ((), ())),
            preferred_element_type=F32,
        )
        rows = pl.ds(pl.multiple_of(at * GROUP * 64, GROUP * 64), GROUP * 64)
        high, low = split(jnp.concatenate(left, axis=0) * cos_ref[rows, :])
        turned = dot(jnp.concatenate([high, low, high], axis=1), pt_ref[...])
        for i in range(GROUP):
            j = at * GROUP + i
            part = turned[i * 64 : (i + 1) * 64]
            cos_sum += part * tc_ref[pl.ds(j, 1), :]
            sin_sum += part * ts_ref[pl.ds(j, 1), :]
        return decay_sum, skip_sum, second, cos_sum, sin_sum

    zero = jnp.zeros((C, B), F32)
    decay_sum, skip_sum, second, cos_sum, sin_sum = lax.fori_loop(
        0,
        J // GROUP,
        reduce_filter,
        (zero, zero, jnp.zeros((64, C), F32), jnp.zeros((64, B), F32), jnp.zeros((64, B), F32)),
    )
    wide[...] = jnp.zeros((B, B), F32)
    wide[:64, :C] = second * scale
    packed = jnp.transpose(wide[...])[:C]
    packed = jnp.where(lane == 64, -scale * jnp.sum(decay_sum, axis=1, keepdims=True), packed)
    packed = jnp.where(lane == 65, scale * jnp.sum(skip_sum, axis=1, keepdims=True), packed)
    gather[my_z, my_y] = packed.astype(BF16)

    lane_64 = lax.broadcasted_iota(jnp.int32, (64, B), 1)
    swapped = jnp.where(lane_64 < 16, pltpu.roll(sin_sum, B - 16, 1), pltpu.roll(sin_sum, 16, 1))
    wide[:64, :] = (cos_sum + swapped) * scale
    wide[64:, :] = jnp.zeros((64, B), F32)
    first = jnp.transpose(wide[...])
    first = jnp.where(lane < 64, first[:16], pltpu.roll(first[16:32], 64, 1))
    for i in range(DEPTH):
        rs_out[i] = first[i : i + 1]
    rs_in[my_z] = rs_out[my_z]

    def send_z(i, carry):
        peer = (my_z + i) % DEPTH
        pltpu.make_async_remote_copy(
            src_ref=rs_out.at[peer],
            dst_ref=rs_in.at[my_z],
            send_sem=send_sem.at[4],
            recv_sem=rz_sem,
            device_id={"seq": peer * PLANE + my_y},
            device_id_type=MESH,
        ).start()
        pltpu.make_async_remote_copy(
            src_ref=gather.at[my_z, my_y],
            dst_ref=gather.at[my_z, my_y],
            send_sem=send_sem.at[5],
            recv_sem=z_sem,
            device_id={"seq": peer * PLANE + my_y},
            device_id_type=MESH,
        ).start()
        return carry

    lax.fori_loop(1, DEPTH, send_z, 0)

    def to_rows(in_ref, at, half):
        block = in_ref[pl.ds(at * 16, 16)].astype(F32)[:, half * 8 : (half + 1) * 8]
        return jnp.transpose(block.reshape(B, B))

    wait_bytes(conv_in, SEQ - 1, cx_sem)

    def rows_q(at, carry):
        for half in range(2):
            lanes = pl.ds(pl.multiple_of(half * 512 + at * B, B), B)
            gq_ref[:, lanes] = (go_ref[:, lanes].astype(F32) * to_rows(conv_in, at, half)).astype(BF16)
        return carry

    lax.fori_loop(0, 4, rows_q, 0)

    wait_bytes(rs_in, DEPTH - 1, rz_sem)
    total = rs_in[0]
    for i in range(1, DEPTH):
        total += rs_in[i]
    plane_in[my_y] = total

    def send_plane(i, carry):
        peer = (my_y + i) % PLANE
        pltpu.make_async_remote_copy(
            src_ref=plane_in.at[my_y],
            dst_ref=plane_in.at[my_y],
            send_sem=send_sem.at[6],
            recv_sem=ry_sem,
            device_id={"seq": my_z * PLANE + peer},
            device_id_type=MESH,
        ).start()
        return carry

    lax.fori_loop(1, PLANE, send_plane, 0)
    wait_bytes(gather.at[:, 0], DEPTH - 1, z_sem)

    def send_gather(i, carry):
        peer = (my_y + i) % PLANE
        pltpu.make_async_remote_copy(
            src_ref=gather.at[:, my_y],
            dst_ref=gather.at[:, my_y],
            send_sem=send_sem.at[7],
            recv_sem=y_sem,
            device_id={"seq": my_z * PLANE + peer},
            device_id_type=MESH,
        ).start()
        return carry

    lax.fori_loop(1, PLANE, send_gather, 0)
    wait_bytes(plane_in, PLANE - 1, ry_sem)
    total = plane_in[0]
    for i in range(1, PLANE):
        total += plane_in[i]
    tp_in[my_tp] = total

    def send_tp(i, carry):
        pltpu.make_async_remote_copy(
            src_ref=tp_in.at[my_tp],
            dst_ref=tp_in.at[my_tp],
            send_sem=send_sem.at[8],
            recv_sem=t_sem,
            device_id={"tp": (my_tp + i) % TP},
            device_id_type=MESH,
        ).start()
        return carry

    lax.fori_loop(1, TP, send_tp, 0)
    wait_bytes(tp_in, TP - 1, t_sem)
    total = tp_in[0]
    for i in range(1, TP):
        total += tp_in[i]
    fin[my_z] = total

    def send_fin(i, carry):
        peer = (my_z + i) % DEPTH
        pltpu.make_async_remote_copy(
            src_ref=fin.at[my_z],
            dst_ref=fin.at[my_z],
            send_sem=send_sem.at[9],
            recv_sem=f_sem,
            device_id={"seq": peer * PLANE + my_y},
            device_id_type=MESH,
        ).start()
        return carry

    lax.fori_loop(1, DEPTH, send_fin, 0)

    wait_bytes(grad_in, SEQ - 1, cg_sem)

    def rows_kv(at, carry):
        for half in range(2):
            lanes = pl.ds(pl.multiple_of(half * 512 + at * B, B), B)
            grad = to_rows(grad_in, at, half)
            gk_ref[:, lanes] = (v_ref[:, lanes].astype(F32) * grad).astype(BF16)
            gv_ref[:, lanes] = (k_ref[:, lanes].astype(F32) * grad).astype(BF16)
        return carry

    lax.fori_loop(0, 4, rows_kv, 0)

    others = gather.at[:, pl.ds(0, PLANE - 1)]
    pltpu.make_async_copy(others, others, y_sem).wait()

    def columns(at, carry):
        for half in range(2):
            lanes = pl.ds(pl.multiple_of(half * 512 + at * B, B), B)
            block = gather[pl.ds(at * 4, 4)].astype(F32).reshape(16, C, B)[:, half * 8 : (half + 1) * 8]
            turned = jnp.transpose(block.reshape(B, B))
            second_ref[:, lanes] = turned[:64]
            gdecay_ref[:, lanes] = turned[64:65]
            gskip_ref[:, lanes] = turned[65:66]
        return carry

    lax.fori_loop(0, 4, columns, 0)

    wait_bytes(fin, DEPTH - 1, f_sem)
    for i in range(DEPTH):
        wide[i : i + 1, :] = fin[i]
    total = wide[:DEPTH, :]
    first_ref[:16, :] = total[:, :64]
    first_ref[16:, :] = pltpu.roll(total, 64, 1)[:, :64]

    for at, ref in enumerate((send_x, send_g, back_x, back_g)):
        wait_bytes(ref, SEQ - 1, send_sem.at[at])
    wait_bytes(rs_out, DEPTH - 1, send_sem.at[4])
    wait_bytes(gather.at[:, 0], DEPTH - 1, send_sem.at[5])
    wait_bytes(plane_in, PLANE - 1, send_sem.at[6])
    pltpu.make_async_copy(others, others, send_sem.at[7]).wait()
    wait_bytes(tp_in, TP - 1, send_sem.at[8])
    wait_bytes(fin, DEPTH - 1, send_sem.at[9])


def per_device(q_proj, k_proj, v_proj, grad_out, w_first, w_second, decay_rate, skip_gain):
    chan = decay_rate.shape[0]
    tables = [jnp.asarray(table) for table in make_tables()]
    rows = jax.ShapeDtypeStruct(q_proj.shape, BF16)
    block = pltpu.VMEM((J, C, B), BF16)
    full = pltpu.VMEM((J * C, B), F32)
    spectrum = pltpu.VMEM((C * J, 2 * B), F32)
    dma = pltpu.SemaphoreType.DMA
    vmem = pl.BlockSpec(memory_space=pltpu.VMEM)
    grad_q, grad_k, grad_v, first, second, decay, skip = pl.pallas_call(
        kernel,
        out_shape=(
            rows,
            rows,
            rows,
            jax.ShapeDtypeStruct(w_first.shape, F32),
            jax.ShapeDtypeStruct(w_second.shape, F32),
            jax.ShapeDtypeStruct((1, chan), F32),
            jax.ShapeDtypeStruct((1, chan), F32),
        ),
        in_specs=[vmem] * (8 + len(tables)),
        out_specs=[vmem] * 7,
        scratch_shapes=[block] * 8
        + [pltpu.VMEM((2, B, B), F32)]
        + [full] * 4
        + [pltpu.VMEM((J * 64, B), BF16)] * 2
        + [pltpu.VMEM((J * 64, B), F32)]
        + [spectrum] * 3
        + [pltpu.VMEM((B, B), F32)]
        + [pltpu.VMEM((DEPTH, PLANE, C, B), BF16)]
        + [pltpu.VMEM((count, 1, B), F32) for count in (DEPTH, DEPTH, PLANE, TP, DEPTH)]
        + [dma((10,))]
        + [dma(())] * 10,
        compiler_params=pltpu.CompilerParams(
            collective_id=0, has_side_effects=True, vmem_limit_bytes=48 * 1024 * 1024
        ),
    )(
        q_proj, k_proj, v_proj, grad_out, w_first, w_second,
        decay_rate.reshape(1, chan), skip_gain.reshape(1, chan), *tables,
    )
    return grad_q, grad_k, grad_v, first, second, decay.reshape(chan), skip.reshape(chan)


def solution(mesh):
    return jax.shard_map(
        per_device,
        mesh=mesh,
        in_specs=(
            P("seq", "tp"),
            P("seq", "tp"),
            P("seq", "tp"),
            P("seq", "tp"),
            P(),
            P(None, "tp"),
            P("tp"),
            P("tp"),
        ),
        out_specs=(
            P("seq", "tp"),
            P("seq", "tp"),
            P("seq", "tp"),
            P(),
            P(None, "tp"),
            P("tp"),
            P("tp"),
        ),
        check_vma=False,
    )
```

```python
import functools
import math

import jax
import jax.numpy as jnp
import numpy as np
from jax import lax
from jax.experimental import pallas as pl
from jax.experimental.pallas import tpu as pltpu
from jax.sharding import PartitionSpec as P

MESH = pl.DeviceIdType.MESH
F32 = jnp.float32
BF16 = jnp.bfloat16
J = 64
B = 128
C = 16
L = J * B
GROUP = 4
SEQ = 64
TP = 8
OPERANDS = 16
DEPTH = 16
PLANE = 4


def split_np(values):
    high = values.astype(np.float32).astype(jnp.bfloat16)
    low = (values - high.astype(np.float64)).astype(np.float32).astype(jnp.bfloat16)
    return high, low


def make_tables():
    turn = 2.0 * math.pi
    k1 = np.arange(J)[:, None] + 0.25
    first = turn * k1 * np.arange(J)[None, :] / J
    f1_high, f1_low = split_np(np.concatenate([np.cos(first), -np.sin(first)], axis=0))
    twiddle = turn * k1 * np.arange(B)[None, :] / L
    second = turn * (np.arange(B)[:, None] * np.arange(B)[None, :] % B) / B
    cos, sin = np.cos(second), np.sin(second)
    f2_high, f2_low = split_np(np.block([[cos, -sin], [sin, cos]]))
    i1_high, i1_low = split_np(np.block([[cos, sin], [-sin, cos]]))
    i2_high, i2_low = split_np(np.concatenate([np.cos(first.T), -np.sin(first.T)], axis=1) / L)
    band = np.arange(16)
    freq = 3 * (band + 1) ** 2 + band
    inner = turn * (freq[:, None] * np.arange(B)[None, :] % L) / L
    p_high, p_low = split_np(np.concatenate([np.sin(inner), np.cos(inner)], axis=0))
    outer = turn * (np.arange(J)[:, None] * freq[None, :] % J) / J
    pos_t = np.zeros((3 * B, B), np.float32).astype(jnp.bfloat16)
    for at, part in enumerate((p_high, p_high, p_low)):
        pos_t[at * B : (at + 1) * B, :32] = part.T
    turn_cos = np.tile(np.concatenate([np.cos(outer), np.cos(outer)], axis=1), (1, 4))
    turn_sin = np.tile(np.concatenate([-np.sin(outer), np.sin(outer)], axis=1), (1, 4))
    return (
        np.concatenate([f1_high, f1_low], axis=1),
        np.concatenate([f1_high, f1_low, f1_high], axis=1),
        np.concatenate([f2_high, f2_high, f2_low], axis=0),
        np.concatenate([i1_high, i1_high, i1_low], axis=0),
        np.concatenate([i2_high, i2_low, i2_high], axis=1),
        np.concatenate([p_high, p_low, p_high, p_low], axis=0),
        pos_t,
        np.stack([np.cos(twiddle), np.sin(twiddle), turn_cos, turn_sin]).astype(np.float32),
    )


def dot(left, right):
    return jnp.dot(left, right, preferred_element_type=F32)


def split(values):
    high = values.astype(BF16)
    return high, (values - high.astype(F32)).astype(BF16)


def sin_cos(x):
    n = jnp.floor(x * (1.0 / math.pi) + 0.5)
    r = (x - n * 3.140625) - n * 9.6765358979e-4
    half = n * 0.5
    sign = 1.0 - 4.0 * (half - jnp.floor(half))
    s = r * r
    p = -1.0 / 39916800.0
    for factor in (1.0 / 362880.0, -1.0 / 5040.0, 1.0 / 120.0, -1.0 / 6.0):
        p = p * s + factor
    sine = (r + r * s * p) * sign
    q = 1.0 / 479001600.0
    for factor in (-1.0 / 3628800.0, 1.0 / 40320.0, -1.0 / 720.0, 1.0 / 24.0, -0.5, 1.0):
        q = q * s + factor
    return sine, q * sign


def kernel(*refs):
    inputs, results, refs = refs[:OPERANDS], refs[OPERANDS : OPERANDS + 7], refs[OPERANDS + 7 :]
    held, refs = refs[:OPERANDS], refs[OPERANDS:]
    outs, refs = refs[:7], refs[7:]
    (
        q_ref, k_ref, v_ref, go_ref, w1_ref, w2_ref, decay_ref, skip_ref,
        f1x_ref, f1_ref, f2_ref, i1_ref, i2_ref, pb_ref, pt_ref, turns_ref,
    ) = held
    gq_ref, gk_ref, gv_ref, first_ref, second_ref, gdecay_ref, gskip_ref = outs
    (
        send_x, send_g, in_x, in_g, back_x, back_g, conv_in, grad_in,
        params, stage, stage_x, raw_ref, env_ref, hid_hi, hid_lo, cos_ref, spec_h, spec_x, spec_g, wide,
        z_in, gather, plane_in, tp_in,
        send_sem, x_sem, g_sem, cx_sem, cg_sem, z_sem, y_sem, ry_sem, t_sem, load_sem, save_sem,
    ) = refs
    twc_ref, tws_ref, tc_ref, ts_ref = (turns_ref.at[i] for i in range(4))

    def load(at):
        return pltpu.make_async_copy(inputs[at], held[at], load_sem.at[at])

    def save(at):
        return pltpu.make_async_copy(outs[at], results[at], save_sem.at[at])

    for at in (1, 2, 0, 3, *range(4, OPERANDS)):
        load(at).start()

    me = lax.axis_index("seq")
    my_tp = lax.axis_index("tp")
    my_z, my_y = me // PLANE, me % PLANE
    scale = L**-0.5

    barrier = pltpu.get_barrier_semaphore()

    def greet(i, carry):
        pl.semaphore_signal(
            barrier, inc=1, device_id={"seq": (me + i) % SEQ}, device_id_type=MESH
        )
        return carry

    lax.fori_loop(1, SEQ, greet, 0)

    def greet_tp(i, carry):
        pl.semaphore_signal(
            barrier, inc=1, device_id={"tp": (my_tp + i) % TP}, device_id_type=MESH
        )
        return carry

    lax.fori_loop(1, TP, greet_tp, 0)

    def gate(left_ref, right_ref, out_ref):
        def step(at, carry):
            parts = []
            for half in range(2):
                lanes = pl.ds(pl.multiple_of(half * 512 + at * B, B), B)
                gated = left_ref[:, lanes].astype(F32) * right_ref[:, lanes].astype(F32)
                parts.append(jnp.transpose(gated).reshape(16, 8, B))
            out_ref[pl.ds(at * 16, 16)] = jnp.concatenate(parts, axis=1).astype(BF16)
            return carry

        lax.fori_loop(0, 4, step, 0)

    def exchange(out_ref, in_ref, recv_sem, send_at, first, last):
        def send(peer):
            pltpu.make_async_remote_copy(
                src_ref=out_ref.at[peer],
                dst_ref=in_ref.at[me],
                send_sem=send_sem.at[send_at],
                recv_sem=recv_sem,
                device_id={"seq": peer},
                device_id_type=MESH,
            ).start()

        def step(i, carry):
            offset = (i * 11) % 32
            send((me + offset) % SEQ)
            send((me + SEQ - offset) % SEQ)
            return carry

        lax.fori_loop(max(first, 1), last, step, 0)
        if first == 0:
            send((me + SEQ // 2) % SEQ)
            in_ref[me] = out_ref[me]

    def wait_bytes(ref, count, sem):
        view = ref.at[pl.ds(0, count)]
        pltpu.make_async_copy(view, view, sem).wait()

    load(1).wait()
    load(2).wait()
    gate(k_ref, v_ref, send_x)
    load(0).wait()
    load(3).wait()
    gate(q_ref, go_ref, send_g)
    pl.semaphore_wait(barrier, SEQ - 1 + TP - 1)
    exchange(send_x, in_x, x_sem, 0, 0, 32)
    for at in range(4, OPERANDS):
        load(at).wait()

    for half in range(2):
        lanes = pl.ds(pl.multiple_of(half * 512 + (me // 16) * B, B), B)
        rows = lax.broadcasted_iota(jnp.int32, (64, B), 0)
        tail = jnp.where(
            rows == 0,
            jnp.broadcast_to(decay_ref[:, lanes], (64, B)),
            jnp.where(rows == 1, jnp.broadcast_to(skip_ref[:, lanes], (64, B)), 0.0),
        )
        params[half] = jnp.transpose(jnp.concatenate([w2_ref[:, lanes], tail], axis=0))
    pick = pl.ds(pl.multiple_of((me % 16) * 8, 8), 8)
    mine = jnp.concatenate([params[0, pick, :], params[1, pick, :]], axis=0)
    lane = lax.broadcasted_iota(jnp.int32, (C, B), 1)
    weights = jnp.where(lane < 64, mine, 0.0)
    decay = jnp.sum(jnp.where(lane == 64, mine, 0.0), axis=1, keepdims=True)
    skip = jnp.sum(jnp.where(lane == 65, mine, 0.0), axis=1, keepdims=True)
    w_high = weights.astype(BF16).astype(F32)
    w_low = (weights - w_high).astype(BF16).astype(F32)
    w_pair = w_high + pltpu.roll(w_low, 64, 1)
    w_rows = jnp.concatenate([w_pair, w_pair], axis=1).astype(BF16)
    wide[...] = jnp.zeros((B, B), F32)
    for at, part in enumerate((w_high, w_low, w_high, w_low)):
        wide[at * C : (at + 1) * C, :] = part
    w_cols = jnp.transpose(wide[...])[:64, :64].astype(BF16)

    w_one = w1_ref[...]
    w_swap = jnp.concatenate([w_one[16:], w_one[:16]], axis=0)
    wide[:, :64] = jnp.concatenate([w_one] * 4, axis=0)
    turned = jnp.transpose(wide[...])[:64]
    wide[:, :64] = jnp.concatenate([w_swap] * 4, axis=0)
    turned_swap = jnp.transpose(wide[...])[:64]
    lane_b = lax.broadcasted_iota(jnp.int32, (GROUP * 64, B), 1)
    position = lax.broadcasted_iota(jnp.int32, (C, B), 1).astype(F32)

    def network(at, carry):
        pieces = []
        for i in range(GROUP):
            j = at * GROUP + i
            pieces.append(turned * tc_ref[pl.ds(j, 1), :] + turned_swap * ts_ref[pl.ds(j, 1), :])
        values = jnp.concatenate(pieces, axis=0)
        high = values.astype(BF16).astype(F32)
        left = jnp.where(lane_b < 64, high, values - high).astype(BF16)
        sine, cosine = sin_cos(dot(left, pb_ref[...]))
        rows = pl.ds(pl.multiple_of(at * GROUP * 64, GROUP * 64), GROUP * 64)
        cos_ref[rows, :] = cosine
        high, low = split(sine)
        hid_hi[rows, :] = high
        hid_lo[rows, :] = low
        for i in range(0, GROUP, 2):
            h = jnp.concatenate([high[i * 64 : (i + 1) * 64], high[(i + 1) * 64 : (i + 2) * 64]], axis=1)
            l = jnp.concatenate([low[i * 64 : (i + 1) * 64], low[(i + 1) * 64 : (i + 2) * 64]], axis=1)
            raw = dot(w_rows, jnp.concatenate([h, h, l, l], axis=0))
            for o in range(2):
                j = at * GROUP + i + o
                fraction = (position + (j * B).astype(F32)) * (1.0 / L)
                envelope = jnp.exp(-decay * fraction) * scale
                part = raw[:, o * B : (o + 1) * B]
                here = pl.ds(pl.multiple_of(j * C, C), C)
                raw_ref[here, :] = part
                env_ref[here, :] = envelope
                stage[here, :] = part * envelope
        return carry

    lax.fori_loop(0, J // GROUP, network, 0)

    def forward(from_ref, spec_ref, exact):
        def step(at, carry):
            cols = [from_ref[pl.ds(at * GROUP + i, J, stride=C), :] for i in range(GROUP)]
            data = jnp.concatenate(cols, axis=1)
            if exact:
                data = data.astype(BF16)
                mixed = dot(f1x_ref[...], jnp.concatenate([data, data], axis=0))
            else:
                high, low = split(data)
                mixed = dot(f1_ref[...], jnp.concatenate([high, high, low], axis=0))
            turned = []
            for i in range(GROUP):
                re, im = mixed[:J, i * B : (i + 1) * B], mixed[J:, i * B : (i + 1) * B]
                c, s = twc_ref[...], tws_ref[...]
                turned.append(jnp.concatenate([re * c + im * s, im * c - re * s], axis=1))
            high, low = split(jnp.concatenate(turned, axis=0))
            rows = pl.ds(pl.multiple_of(at * GROUP * J, GROUP * J), GROUP * J)
            spec_ref[rows, :] = dot(jnp.concatenate([high, low, high], axis=1), f2_ref[...])
            return carry

        lax.fori_loop(0, C // GROUP, step, 0)

    def inverse(left_ref, right_ref, conjugate):
        def step(at, carry):
            rows = pl.ds(pl.multiple_of(at * GROUP * J, GROUP * J), GROUP * J)
            a, b = left_ref[rows, :], right_ref[rows, :]
            ar, ai, br, bi = a[:, :B], a[:, B:], b[:, :B], b[:, B:]
            if conjugate:
                product = jnp.concatenate([ar * br + ai * bi, ar * bi - ai * br], axis=1)
            else:
                product = jnp.concatenate([ar * br - ai * bi, ar * bi + ai * br], axis=1)
            high, low = split(product)
            mixed = dot(jnp.concatenate([high, low, high], axis=1), i1_ref[...])
            turned = []
            for i in range(GROUP):
                re, im = mixed[i * J : (i + 1) * J, :B], mixed[i * J : (i + 1) * J, B:]
                c, s = twc_ref[...], tws_ref[...]
                turned.append(jnp.concatenate([re * c - im * s, re * s + im * c], axis=0))
            high, low = split(jnp.concatenate(turned, axis=1))
            result = dot(i2_ref[...], jnp.concatenate([high, high, low], axis=0))
            for i in range(GROUP):
                stage[pl.ds(at * GROUP + i, J, stride=C), :] = result[:, i * B : (i + 1) * B]
            return carry

        lax.fori_loop(0, C // GROUP, step, 0)

    def finish(in_ref, out_ref):
        def step(at, carry):
            blocks = pl.ds(at * 8, 8)
            rows = pl.ds(pl.multiple_of(at * 8 * C, 8 * C), 8 * C)
            values = stage[rows, :].reshape(8, C, B) + skip[None] * in_ref[blocks].astype(F32)
            out_ref[blocks] = values.astype(BF16)
            return carry

        lax.fori_loop(0, J // 8, step, 0)

    def widen(in_ref, to_ref):
        def step(at, carry):
            rows = pl.ds(pl.multiple_of(at * 8 * C, 8 * C), 8 * C)
            to_ref[rows, :] = in_ref[pl.ds(at * 8, 8)].astype(F32).reshape(8 * C, B)
            return carry

        lax.fori_loop(0, J // 8, step, 0)

    forward(stage, spec_h, False)
    exchange(send_g, in_g, g_sem, 1, 0, 32)
    wait_bytes(in_x, SEQ - 1, x_sem)
    widen(in_x, stage_x)
    forward(stage_x, spec_x, True)
    inverse(spec_h, spec_x, False)
    finish(in_x, back_x)
    exchange(back_x, conv_in, cx_sem, 2, 0, 32)

    wait_bytes(in_g, SEQ - 1, g_sem)
    widen(in_g, stage)
    forward(stage, spec_g, True)
    inverse(spec_x, spec_g, True)

    def reduce_filter(at, carry):
        decay_sum, skip_sum, second, cos_sum, sin_sum = carry
        left, right, hid_rows = [], [], []
        for i in range(GROUP):
            j = at * GROUP + i
            here = pl.ds(pl.multiple_of(j * C, C), C)
            grad_raw = stage[here, :] * env_ref[here, :]
            fraction = (position + (j * B).astype(F32)) * (1.0 / L)
            decay_sum += grad_raw * raw_ref[here, :] * fraction
            skip_sum += in_x[j].astype(F32) * in_g[j].astype(F32)
            high, low = split(grad_raw)
            right.append(jnp.concatenate([high, high, low], axis=1))
            rows = pl.ds(pl.multiple_of(j * 64, 64), 64)
            h = hid_hi[rows, :]
            hid_rows.append(jnp.concatenate([h, hid_lo[rows, :], h], axis=1))
            left.append(dot(w_cols, jnp.concatenate([high, high, low, low], axis=0)))
        second += lax.dot_general(
            jnp.concatenate(hid_rows, axis=1),
            jnp.concatenate(right, axis=1),
            (((1,), (1,)), ((), ())),
            preferred_element_type=F32,
        )
        rows = pl.ds(pl.multiple_of(at * GROUP * 64, GROUP * 64), GROUP * 64)
        high, low = split(jnp.concatenate(left, axis=0) * cos_ref[rows, :])
        turned = dot(jnp.concatenate([high, low, high], axis=1), pt_ref[...])
        for i in range(GROUP):
            j = at * GROUP + i
            part = turned[i * 64 : (i + 1) * 64]
            cos_sum += part * tc_ref[pl.ds(j, 1), :]
            sin_sum += part * ts_ref[pl.ds(j, 1), :]
        return decay_sum, skip_sum, second, cos_sum, sin_sum

    zero = jnp.zeros((C, B), F32)
    decay_sum, skip_sum, second, cos_sum, sin_sum = lax.fori_loop(
        0,
        J // GROUP,
        reduce_filter,
        (zero, zero, jnp.zeros((64, C), F32), jnp.zeros((64, B), F32), jnp.zeros((64, B), F32)),
    )
    wide[...] = jnp.zeros((B, B), F32)
    wide[:64, :C] = second * scale
    packed = jnp.transpose(wide[...])[:C]
    packed = jnp.where(lane == 64, -scale * jnp.sum(decay_sum, axis=1, keepdims=True), packed)
    packed = jnp.where(lane == 65, scale * jnp.sum(skip_sum, axis=1, keepdims=True), packed)
    z_in[my_z, 0] = packed.astype(BF16)

    lane_64 = lax.broadcasted_iota(jnp.int32, (64, B), 1)
    swapped = jnp.where(lane_64 < 16, pltpu.roll(sin_sum, B - 16, 1), pltpu.roll(sin_sum, 16, 1))
    wide[:64, :] = (cos_sum + swapped) * scale
    wide[64:, :] = jnp.zeros((64, B), F32)
    first = jnp.transpose(wide[...])
    first = jnp.where(lane < 64, first[:16], pltpu.roll(first[16:32], 64, 1))
    z_in[my_z, 1] = first.astype(BF16)

    def spread(ref, mine, sem, send_at, count, peer_of):
        def step(i, carry):
            pltpu.make_async_remote_copy(
                src_ref=ref.at[mine],
                dst_ref=ref.at[mine],
                send_sem=send_sem.at[send_at],
                recv_sem=sem,
                device_id=peer_of((mine + i) % count),
                device_id_type=MESH,
            ).start()
            return carry

        lax.fori_loop(1, count, step, 0)

    def on_plane(peer):
        return {"seq": my_z * PLANE + peer}

    spread(z_in, my_z, z_sem, 4, DEPTH, lambda peer: {"seq": peer * PLANE + my_y})
    inverse(spec_h, spec_g, True)
    finish(in_g, back_g)
    exchange(back_g, grad_in, cg_sem, 3, 0, 32)

    def to_rows(in_ref, at, half):
        block = in_ref[pl.ds(at * 16, 16)].astype(F32)[:, half * 8 : (half + 1) * 8]
        return jnp.transpose(block.reshape(B, B))

    wait_bytes(z_in, DEPTH - 1, z_sem)
    total = z_in[0, 1].astype(F32)
    for i in range(1, DEPTH):
        total += z_in[i, 1].astype(F32)
    plane_in[my_y] = total
    spread(plane_in, my_y, ry_sem, 6, PLANE, on_plane)
    gather[my_y] = z_in[:, 0]
    spread(gather, my_y, y_sem, 5, PLANE, on_plane)
    wait_bytes(conv_in, SEQ - 1, cx_sem)

    def rows_q(at, carry):
        for half in range(2):
            lanes = pl.ds(pl.multiple_of(half * 512 + at * B, B), B)
            gq_ref[:, lanes] = (go_ref[:, lanes].astype(F32) * to_rows(conv_in, at, half)).astype(BF16)
        return carry

    lax.fori_loop(0, 4, rows_q, 0)

    save(0).start()
    wait_bytes(plane_in, PLANE - 1, ry_sem)
    total = plane_in[0]
    for i in range(1, PLANE):
        total += plane_in[i]
    tp_in[my_tp] = total
    spread(tp_in, my_tp, t_sem, 7, TP, lambda peer: {"tp": peer})
    wait_bytes(gather, PLANE - 1, y_sem)

    def columns(at, carry):
        for half in range(2):
            lanes = pl.ds(pl.multiple_of(half * 512 + at * B, B), B)
            parts = [
                gather[y, at * 4 + z].astype(F32)[half * 8 : (half + 1) * 8]
                for z in range(4)
                for y in range(PLANE)
            ]
            turned = jnp.transpose(jnp.concatenate(parts, axis=0))
            second_ref[:, lanes] = turned[:64]
            gdecay_ref[:, lanes] = turned[64:65]
            gskip_ref[:, lanes] = turned[65:66]
        return carry

    lax.fori_loop(0, 4, columns, 0)
    wait_bytes(tp_in, TP - 1, t_sem)
    total = tp_in[0]
    for i in range(1, TP):
        total += tp_in[i]
    first_ref[:16, :] = total[:, :64]
    first_ref[16:, :] = pltpu.roll(total, 64, 1)[:, :64]
    for at in range(3, 7):
        save(at).start()

    wait_bytes(grad_in, SEQ - 1, cg_sem)

    def rows_kv(at, carry):
        for half in range(2):
            lanes = pl.ds(pl.multiple_of(half * 512 + at * B, B), B)
            grad = to_rows(grad_in, at, half)
            gk_ref[:, lanes] = (v_ref[:, lanes].astype(F32) * grad).astype(BF16)
            gv_ref[:, lanes] = (k_ref[:, lanes].astype(F32) * grad).astype(BF16)
        return carry

    lax.fori_loop(0, 4, rows_kv, 0)
    save(1).start()
    save(2).start()

    for at, ref in enumerate((send_x, send_g, back_x, back_g)):
        wait_bytes(ref, SEQ - 1, send_sem.at[at])
    wait_bytes(z_in, DEPTH - 1, send_sem.at[4])
    wait_bytes(gather, PLANE - 1, send_sem.at[5])
    wait_bytes(plane_in, PLANE - 1, send_sem.at[6])
    wait_bytes(tp_in, TP - 1, send_sem.at[7])
    for at in range(7):
        save(at).wait()


def copy_kernel(*refs):
    sources, targets, held, load_sem, save_sem = refs[:7], refs[7:14], refs[14:21], refs[21], refs[22]
    loads = [pltpu.make_async_copy(sources[i], held[i], load_sem.at[i]) for i in range(7)]
    saves = [pltpu.make_async_copy(held[i], targets[i], save_sem.at[i]) for i in range(7)]
    for copy in loads:
        copy.start()
    for load, copy in zip(loads, saves):
        load.wait()
        copy.start()
    for copy in saves:
        copy.wait()


def per_device(q_proj, k_proj, v_proj, grad_out, w_first, w_second, decay_rate, skip_gain):
    chan = decay_rate.shape[0]
    tables = [jnp.asarray(table) for table in make_tables()]
    rows = jax.ShapeDtypeStruct(q_proj.shape, BF16)
    block = pltpu.VMEM((J, C, B), BF16)
    full = pltpu.VMEM((J * C, B), F32)
    spectrum = pltpu.VMEM((C * J, 2 * B), F32)
    dma = pltpu.SemaphoreType.DMA
    anywhere = pl.BlockSpec(memory_space=pl.ANY)
    operands = (
        q_proj, k_proj, v_proj, grad_out, w_first, w_second,
        decay_rate.reshape(1, chan), skip_gain.reshape(1, chan), *tables,
    )
    shapes = (
        rows,
        rows,
        rows,
        jax.ShapeDtypeStruct(w_first.shape, F32),
        jax.ShapeDtypeStruct(w_second.shape, F32),
        jax.ShapeDtypeStruct((1, chan), F32),
        jax.ShapeDtypeStruct((1, chan), F32),
    )
    results = pl.pallas_call(
        kernel,
        out_shape=shapes,
        in_specs=[anywhere] * OPERANDS,
        out_specs=[anywhere] * 7,
        scratch_shapes=[pltpu.VMEM(x.shape, x.dtype) for x in (*operands, *shapes)]
        + [block] * 8
        + [pltpu.VMEM((2, B, B), F32)]
        + [full] * 4
        + [pltpu.VMEM((J * 64, B), BF16)] * 2
        + [pltpu.VMEM((J * 64, B), F32)]
        + [spectrum] * 3
        + [pltpu.VMEM((B, B), F32)]
        + [pltpu.VMEM((DEPTH, 2, C, B), BF16), pltpu.VMEM((PLANE, DEPTH, C, B), BF16)]
        + [pltpu.VMEM((count, C, B), F32) for count in (PLANE, TP)]
        + [dma((8,))]
        + [dma(())] * 8
        + [dma((OPERANDS,)), dma((7,))],
        compiler_params=pltpu.CompilerParams(
            collective_id=0, has_side_effects=True, vmem_limit_bytes=56 * 1024 * 1024
        ),
    )(*operands)
    grad_q, grad_k, grad_v, first, second, decay, skip = pl.pallas_call(
        copy_kernel,
        out_shape=shapes,
        in_specs=[anywhere] * 7,
        out_specs=[anywhere] * 7,
        scratch_shapes=[pltpu.VMEM(x.shape, x.dtype) for x in shapes] + [dma((7,))] * 2,
    )(*results)
    return grad_q, grad_k, grad_v, first, second, decay.reshape(chan), skip.reshape(chan)


def solution(mesh):
    return jax.shard_map(
        per_device,
        mesh=mesh,
        in_specs=(
            P("seq", "tp"),
            P("seq", "tp"),
            P("seq", "tp"),
            P("seq", "tp"),
            P(),
            P(None, "tp"),
            P("tp"),
            P("tp"),
        ),
        out_specs=(
            P("seq", "tp"),
            P("seq", "tp"),
            P("seq", "tp"),
            P(),
            P(None, "tp"),
            P("tp"),
            P("tp"),
        ),
        check_vma=False,
    )
```

```python
import functools
import math

import jax
import jax.numpy as jnp
import numpy as np
from jax import lax
from jax.experimental import pallas as pl
from jax.experimental.pallas import tpu as pltpu
from jax.sharding import PartitionSpec as P

MESH = pl.DeviceIdType.MESH
F32 = jnp.float32
BF16 = jnp.bfloat16
J = 64
B = 128
C = 16
L = J * B
GROUP = 16
NET = 16
RED = 16
SEQ = 64
TP = 8
OPERANDS = 16
DEPTH = 16
PLANE = 4


def split_np(values):
    high = values.astype(np.float32).astype(jnp.bfloat16)
    low = (values - high.astype(np.float64)).astype(np.float32).astype(jnp.bfloat16)
    return high, low


def make_tables():
    turn = 2.0 * math.pi
    k1 = np.arange(J)[:, None] + 0.25
    first = turn * k1 * np.arange(J)[None, :] / J
    f1_high, f1_low = split_np(np.concatenate([np.cos(first), -np.sin(first)], axis=0))
    twiddle = turn * k1 * np.arange(B)[None, :] / L
    second = turn * (np.arange(B)[:, None] * np.arange(B)[None, :] % B) / B
    cos, sin = np.cos(second), np.sin(second)
    f2_high, f2_low = split_np(np.block([[cos, -sin], [sin, cos]]))
    i1_high, i1_low = split_np(np.block([[cos, sin], [-sin, cos]]))
    i2_high, i2_low = split_np(np.concatenate([np.cos(first.T), -np.sin(first.T)], axis=1) / L)
    band = np.arange(16)
    freq = 3 * (band + 1) ** 2 + band
    inner = turn * (freq[:, None] * np.arange(B)[None, :] % L) / L
    p_high, p_low = split_np(np.concatenate([np.sin(inner), np.cos(inner)], axis=0))
    outer = turn * (np.arange(J)[:, None] * freq[None, :] % J) / J
    pos_t = np.zeros((3 * B, B), np.float32).astype(jnp.bfloat16)
    for at, part in enumerate((p_high, p_high, p_low)):
        pos_t[at * B : (at + 1) * B, :32] = part.T
    turn_cos = np.tile(np.concatenate([np.cos(outer), np.cos(outer)], axis=1), (1, 4))
    turn_sin = np.tile(np.concatenate([-np.sin(outer), np.sin(outer)], axis=1), (1, 4))
    return (
        np.concatenate([f1_high, f1_low], axis=1),
        np.concatenate([f1_high, f1_low, f1_high], axis=1),
        np.concatenate([f2_high, f2_high, f2_low], axis=0),
        np.concatenate([i1_high, i1_high, i1_low], axis=0),
        np.concatenate([i2_high, i2_low, i2_high], axis=1),
        np.concatenate([p_high, p_low, p_high, p_low], axis=0),
        pos_t,
        np.stack([np.cos(twiddle), np.sin(twiddle), turn_cos, turn_sin]).astype(np.float32),
    )


def dot(left, right):
    return jnp.dot(left, right, preferred_element_type=F32)


def split(values):
    high = values.astype(BF16)
    return high, (values - high.astype(F32)).astype(BF16)


def sin_cos(x):
    n = jnp.floor(x * (1.0 / math.pi) + 0.5)
    r = (x - n * 3.140625) - n * 9.6765358979e-4
    half = n * 0.5
    sign = 1.0 - 4.0 * (half - jnp.floor(half))
    s = r * r
    p = -1.0 / 39916800.0
    for factor in (1.0 / 362880.0, -1.0 / 5040.0, 1.0 / 120.0, -1.0 / 6.0):
        p = p * s + factor
    sine = (r + r * s * p) * sign
    q = 1.0 / 479001600.0
    for factor in (-1.0 / 3628800.0, 1.0 / 40320.0, -1.0 / 720.0, 1.0 / 24.0, -0.5, 1.0):
        q = q * s + factor
    return sine, q * sign


def kernel(*refs):
    inputs, outs, refs = refs[:OPERANDS], refs[OPERANDS : OPERANDS + 7], refs[OPERANDS + 7 :]
    held, refs = refs[:OPERANDS], refs[OPERANDS:]
    (
        q_ref, k_ref, v_ref, go_ref, w1_ref, w2_ref, decay_ref, skip_ref,
        f1x_ref, f1_ref, f2_ref, i1_ref, i2_ref, pb_ref, pt_ref, turns_ref,
    ) = held
    gq_ref, gk_ref, gv_ref, first_ref, second_ref, gdecay_ref, gskip_ref = outs
    (
        send_x, send_g, in_x, in_g, back_x, back_g, conv_in, grad_in,
        params, stage, stage_x, raw_ref, env_ref, hid_hi, hid_lo, cos_ref, spec_h, spec_x, spec_g, wide,
        z_in, gather, rs_out, rs_in, plane_in, tp_in, fin,
        send_sem, x_sem, g_sem, cx_sem, cg_sem, z_sem, rz_sem, y_sem, ry_sem, t_sem, f_sem, load_sem,
    ) = refs
    twc_ref, tws_ref, tc_ref, ts_ref = (turns_ref.at[i] for i in range(4))

    def load(at):
        return pltpu.make_async_copy(inputs[at], held[at], load_sem.at[at])

    for at in (1, 2, 0, 3, *range(4, OPERANDS)):
        load(at).start()

    me = lax.axis_index("seq")
    my_tp = lax.axis_index("tp")
    my_z, my_y = me // PLANE, me % PLANE
    scale = L**-0.5

    barrier = pltpu.get_barrier_semaphore()

    def greet(i, carry):
        pl.semaphore_signal(
            barrier, inc=1, device_id={"seq": (me + i) % SEQ}, device_id_type=MESH
        )
        return carry

    lax.fori_loop(1, SEQ, greet, 0)

    def greet_tp(i, carry):
        pl.semaphore_signal(
            barrier, inc=1, device_id={"tp": (my_tp + i) % TP}, device_id_type=MESH
        )
        return carry

    lax.fori_loop(1, TP, greet_tp, 0)

    def gate(left_ref, right_ref, out_ref):
        def step(at, carry):
            parts = []
            for half in range(2):
                lanes = pl.ds(pl.multiple_of(half * 512 + at * B, B), B)
                gated = left_ref[:, lanes].astype(F32) * right_ref[:, lanes].astype(F32)
                parts.append(jnp.transpose(gated).reshape(16, 8, B))
            out_ref[pl.ds(at * 16, 16)] = jnp.concatenate(parts, axis=1).astype(BF16)
            return carry

        lax.fori_loop(0, 4, step, 0)

    def exchange(out_ref, in_ref, recv_sem, send_at, first, last):
        def send(peer):
            pltpu.make_async_remote_copy(
                src_ref=out_ref.at[peer],
                dst_ref=in_ref.at[me],
                send_sem=send_sem.at[send_at],
                recv_sem=recv_sem,
                device_id={"seq": peer},
                device_id_type=MESH,
            ).start()

        def step(i, carry):
            offset = (i * 11) % 32
            send((me + offset) % SEQ)
            send((me + SEQ - offset) % SEQ)
            return carry

        lax.fori_loop(max(first, 1), last, step, 0)
        if first == 0:
            send((me + SEQ // 2) % SEQ)
            in_ref[me] = out_ref[me]

    def wait_bytes(ref, count, sem):
        view = ref.at[pl.ds(0, count)]
        pltpu.make_async_copy(view, view, sem).wait()

    load(1).wait()
    load(2).wait()
    gate(k_ref, v_ref, send_x)
    pl.semaphore_wait(barrier, SEQ - 1 + TP - 1)
    exchange(send_x, in_x, x_sem, 0, 0, 32)
    load(0).wait()
    load(3).wait()
    gate(q_ref, go_ref, send_g)
    for at in range(4, OPERANDS):
        load(at).wait()

    for half in range(2):
        lanes = pl.ds(pl.multiple_of(half * 512 + (me // 16) * B, B), B)
        rows = lax.broadcasted_iota(jnp.int32, (64, B), 0)
        tail = jnp.where(
            rows == 0,
            jnp.broadcast_to(decay_ref[:, lanes], (64, B)),
            jnp.where(rows == 1, jnp.broadcast_to(skip_ref[:, lanes], (64, B)), 0.0),
        )
        params[half] = jnp.transpose(jnp.concatenate([w2_ref[:, lanes], tail], axis=0))
    pick = pl.ds(pl.multiple_of((me % 16) * 8, 8), 8)
    mine = jnp.concatenate([params[0, pick, :], params[1, pick, :]], axis=0)
    lane = lax.broadcasted_iota(jnp.int32, (C, B), 1)
    weights = jnp.where(lane < 64, mine, 0.0)
    decay = jnp.sum(jnp.where(lane == 64, mine, 0.0), axis=1, keepdims=True)
    skip = jnp.sum(jnp.where(lane == 65, mine, 0.0), axis=1, keepdims=True)
    w_high = weights.astype(BF16).astype(F32)
    w_low = (weights - w_high).astype(BF16).astype(F32)
    w_pair = w_high + pltpu.roll(w_low, 64, 1)
    w_rows = jnp.concatenate([w_pair, w_pair], axis=1).astype(BF16)
    wide[...] = jnp.zeros((B, B), F32)
    for at, part in enumerate((w_high, w_low, w_high, w_low)):
        wide[at * C : (at + 1) * C, :] = part
    w_cols = jnp.transpose(wide[...])[:64, :64].astype(BF16)

    w_one = w1_ref[...]
    w_swap = jnp.concatenate([w_one[16:], w_one[:16]], axis=0)
    wide[:, :64] = jnp.concatenate([w_one] * 4, axis=0)
    turned = jnp.transpose(wide[...])[:64]
    wide[:, :64] = jnp.concatenate([w_swap] * 4, axis=0)
    turned_swap = jnp.transpose(wide[...])[:64]
    lane_b = lax.broadcasted_iota(jnp.int32, (NET * 64, B), 1)
    position = lax.broadcasted_iota(jnp.int32, (C, B), 1).astype(F32)

    def network(at, carry):
        pieces = []
        for i in range(NET):
            j = at * NET + i
            pieces.append(turned * tc_ref[pl.ds(j, 1), :] + turned_swap * ts_ref[pl.ds(j, 1), :])
        values = jnp.concatenate(pieces, axis=0)
        high = values.astype(BF16).astype(F32)
        left = jnp.where(lane_b < 64, high, values - high).astype(BF16)
        sine, cosine = sin_cos(dot(left, pb_ref[...]))
        rows = pl.ds(pl.multiple_of(at * NET * 64, NET * 64), NET * 64)
        cos_ref[rows, :] = cosine
        high, low = split(sine)
        hid_hi[rows, :] = high
        hid_lo[rows, :] = low
        for i in range(0, NET, 2):
            h = jnp.concatenate([high[i * 64 : (i + 1) * 64], high[(i + 1) * 64 : (i + 2) * 64]], axis=1)
            l = jnp.concatenate([low[i * 64 : (i + 1) * 64], low[(i + 1) * 64 : (i + 2) * 64]], axis=1)
            raw = dot(w_rows, jnp.concatenate([h, h, l, l], axis=0))
            for o in range(2):
                j = at * NET + i + o
                fraction = (position + (j * B).astype(F32)) * (1.0 / L)
                envelope = jnp.exp(-decay * fraction) * scale
                part = raw[:, o * B : (o + 1) * B]
                here = pl.ds(pl.multiple_of(j * C, C), C)
                raw_ref[here, :] = part
                env_ref[here, :] = envelope
                stage[here, :] = part * envelope
        return carry

    lax.fori_loop(0, J // NET, network, 0)

    def forward(from_ref, spec_ref, exact):
        def step(at, carry):
            cols = [from_ref[pl.ds(at * GROUP + i, J, stride=C), :] for i in range(GROUP)]
            data = jnp.concatenate(cols, axis=1)
            if exact:
                data = data.astype(BF16)
                mixed = dot(f1x_ref[...], jnp.concatenate([data, data], axis=0))
            else:
                high, low = split(data)
                mixed = dot(f1_ref[...], jnp.concatenate([high, high, low], axis=0))
            turned = []
            for i in range(GROUP):
                re, im = mixed[:J, i * B : (i + 1) * B], mixed[J:, i * B : (i + 1) * B]
                c, s = twc_ref[...], tws_ref[...]
                turned.append(jnp.concatenate([re * c + im * s, im * c - re * s], axis=1))
            high, low = split(jnp.concatenate(turned, axis=0))
            rows = pl.ds(pl.multiple_of(at * GROUP * J, GROUP * J), GROUP * J)
            spec_ref[rows, :] = dot(jnp.concatenate([high, low, high], axis=1), f2_ref[...])
            return carry

        lax.fori_loop(0, C // GROUP, step, 0)

    def inverse(left_ref, right_ref, conjugate):
        def step(at, carry):
            rows = pl.ds(pl.multiple_of(at * GROUP * J, GROUP * J), GROUP * J)
            a, b = left_ref[rows, :], right_ref[rows, :]
            ar, ai, br, bi = a[:, :B], a[:, B:], b[:, :B], b[:, B:]
            if conjugate:
                product = jnp.concatenate([ar * br + ai * bi, ar * bi - ai * br], axis=1)
            else:
                product = jnp.concatenate([ar * br - ai * bi, ar * bi + ai * br], axis=1)
            high, low = split(product)
            mixed = dot(jnp.concatenate([high, low, high], axis=1), i1_ref[...])
            turned = []
            for i in range(GROUP):
                re, im = mixed[i * J : (i + 1) * J, :B], mixed[i * J : (i + 1) * J, B:]
                c, s = twc_ref[...], tws_ref[...]
                turned.append(jnp.concatenate([re * c - im * s, re * s + im * c], axis=0))
            high, low = split(jnp.concatenate(turned, axis=1))
            result = dot(i2_ref[...], jnp.concatenate([high, high, low], axis=0))
            for i in range(GROUP):
                stage[pl.ds(at * GROUP + i, J, stride=C), :] = result[:, i * B : (i + 1) * B]
            return carry

        lax.fori_loop(0, C // GROUP, step, 0)

    def finish(in_ref, out_ref):
        def step(at, carry):
            blocks = pl.ds(at * 8, 8)
            rows = pl.ds(pl.multiple_of(at * 8 * C, 8 * C), 8 * C)
            values = stage[rows, :].reshape(8, C, B) + skip[None] * in_ref[blocks].astype(F32)
            out_ref[blocks] = values.astype(BF16)
            return carry

        lax.fori_loop(0, J // 8, step, 0)

    def widen(in_ref, to_ref):
        def step(at, carry):
            rows = pl.ds(pl.multiple_of(at * 8 * C, 8 * C), 8 * C)
            to_ref[rows, :] = in_ref[pl.ds(at * 8, 8)].astype(F32).reshape(8 * C, B)
            return carry

        lax.fori_loop(0, J // 8, step, 0)

    forward(stage, spec_h, False)
    exchange(send_g, in_g, g_sem, 1, 0, 32)
    wait_bytes(in_x, SEQ - 1, x_sem)
    widen(in_x, stage_x)
    forward(stage_x, spec_x, True)
    inverse(spec_h, spec_x, False)
    finish(in_x, back_x)
    exchange(back_x, conv_in, cx_sem, 2, 0, 32)

    wait_bytes(in_g, SEQ - 1, g_sem)
    widen(in_g, stage)
    forward(stage, spec_g, True)
    inverse(spec_h, spec_g, True)
    finish(in_g, back_g)
    exchange(back_g, grad_in, cg_sem, 3, 0, 4)
    inverse(spec_x, spec_g, True)

    def reduce_filter(at, carry):
        decay_sum, skip_sum, second, cos_sum, sin_sum = carry
        left, right, hid_rows = [], [], []
        for i in range(RED):
            j = at * RED + i
            here = pl.ds(pl.multiple_of(j * C, C), C)
            grad_raw = stage[here, :] * env_ref[here, :]
            fraction = (position + (j * B).astype(F32)) * (1.0 / L)
            decay_sum += grad_raw * raw_ref[here, :] * fraction
            skip_sum += in_x[j].astype(F32) * in_g[j].astype(F32)
            high, low = split(grad_raw)
            right.append(jnp.concatenate([high, high, low], axis=1))
            rows = pl.ds(pl.multiple_of(j * 64, 64), 64)
            h = hid_hi[rows, :]
            hid_rows.append(jnp.concatenate([h, hid_lo[rows, :], h], axis=1))
            left.append(dot(w_cols, jnp.concatenate([high, high, low, low], axis=0)))
        second += lax.dot_general(
            jnp.concatenate(hid_rows, axis=1),
            jnp.concatenate(right, axis=1),
            (((1,), (1,)), ((), ())),
            preferred_element_type=F32,
        )
        rows = pl.ds(pl.multiple_of(at * RED * 64, RED * 64), RED * 64)
        high, low = split(jnp.concatenate(left, axis=0) * cos_ref[rows, :])
        turned = dot(jnp.concatenate([high, low, high], axis=1), pt_ref[...])
        for i in range(RED):
            j = at * RED + i
            part = turned[i * 64 : (i + 1) * 64]
            cos_sum += part * tc_ref[pl.ds(j, 1), :]
            sin_sum += part * ts_ref[pl.ds(j, 1), :]
        return decay_sum, skip_sum, second, cos_sum, sin_sum

    zero = jnp.zeros((C, B), F32)
    decay_sum, skip_sum, second, cos_sum, sin_sum = lax.fori_loop(
        0,
        J // RED,
        reduce_filter,
        (zero, zero, jnp.zeros((64, C), F32), jnp.zeros((64, B), F32), jnp.zeros((64, B), F32)),
    )
    wide[...] = jnp.zeros((B, B), F32)
    wide[:64, :C] = second * scale
    packed = jnp.transpose(wide[...])[:C]
    packed = jnp.where(lane[:8] < 64, packed[:8], pltpu.roll(packed[8:], 64, 1))
    row = lax.broadcasted_iota(jnp.int32, (C, B), 0)
    sums = jnp.where(lane == row, -scale * jnp.sum(decay_sum, axis=1, keepdims=True), 0.0)
    sums += jnp.where(lane == row + C, scale * jnp.sum(skip_sum, axis=1, keepdims=True), 0.0)
    sums = jnp.sum(sums, axis=0, keepdims=True)

    lane_64 = lax.broadcasted_iota(jnp.int32, (64, B), 1)
    swapped = jnp.where(lane_64 < 16, pltpu.roll(sin_sum, B - 16, 1), pltpu.roll(sin_sum, 16, 1))
    wide[:64, :] = (cos_sum + swapped) * scale
    wide[64:, :] = jnp.zeros((64, B), F32)
    first = jnp.transpose(wide[...])
    first = jnp.where(lane < 64, first[:16], pltpu.roll(first[16:32], 64, 1))
    for i in range(DEPTH):
        rs_out[i] = first[i : i + 1]
    rs_in[my_z] = rs_out[my_z]
    wide[:8, :] = packed
    wide[8:9, :] = sums
    wide[9:16, :] = jnp.zeros((7, B), F32)
    z_in[my_z] = wide[:C, :].astype(BF16)

    def spread(ref, mine, sem, send_at, count, peer_of, parts=None):
        def step(i, carry):
            peer = (mine + i) % count
            pltpu.make_async_remote_copy(
                src_ref=ref.at[mine] if parts is None else parts.at[peer],
                dst_ref=ref.at[mine],
                send_sem=send_sem.at[send_at],
                recv_sem=sem,
                device_id=peer_of(peer),
                device_id_type=MESH,
            ).start()
            return carry

        lax.fori_loop(1, count, step, 0)

    def on_plane(peer):
        return {"seq": my_z * PLANE + peer}

    def on_depth(peer):
        return {"seq": peer * PLANE + my_y}

    spread(rs_in, my_z, rz_sem, 4, DEPTH, on_depth, rs_out)
    spread(z_in, my_z, z_sem, 5, DEPTH, on_depth)
    exchange(back_g, grad_in, cg_sem, 3, 4, 32)

    def to_rows(in_ref, at, half):
        block = in_ref[pl.ds(at * 16, 16)].astype(F32)[:, half * 8 : (half + 1) * 8]
        return jnp.transpose(block.reshape(B, B))

    def add(ref, count):
        total = ref[0]
        for i in range(1, count):
            total += ref[i]
        return total

    wait_bytes(rs_in, DEPTH - 1, rz_sem)
    plane_in[my_y] = add(rs_in, DEPTH)
    spread(plane_in, my_y, ry_sem, 6, PLANE, on_plane)
    wait_bytes(z_in, DEPTH - 1, z_sem)
    gather[my_y] = z_in[...]
    spread(gather, my_y, y_sem, 7, PLANE, on_plane)
    wait_bytes(plane_in, PLANE - 1, ry_sem)
    tp_in[my_tp] = add(plane_in, PLANE)
    spread(tp_in, my_tp, t_sem, 8, TP, lambda peer: {"tp": peer})
    wait_bytes(conv_in, SEQ - 1, cx_sem)

    def rows_q(at, carry):
        for half in range(2):
            lanes = pl.ds(pl.multiple_of(half * 512 + at * B, B), B)
            gq_ref[:, lanes] = (go_ref[:, lanes].astype(F32) * to_rows(conv_in, at, half)).astype(BF16)
        return carry

    lax.fori_loop(0, 4, rows_q, 0)

    wait_bytes(tp_in, TP - 1, t_sem)
    fin[my_z] = add(tp_in, TP)
    spread(fin, my_z, f_sem, 9, DEPTH, on_depth)
    wait_bytes(gather, PLANE - 1, y_sem)

    source = lax.broadcasted_iota(jnp.int32, (B, 4 * B), 0)
    target = lax.broadcasted_iota(jnp.int32, (B, 4 * B), 1)
    pick = jnp.where(source == target // B * 8 + target % 8, 1.0, 0.0).astype(BF16)
    own = lane // 8 == lax.broadcasted_iota(jnp.int32, (C, B), 0)

    def columns(at, carry):
        tiles = [gather[y, at * 4 + z].astype(F32) for z in range(4) for y in range(PLANE)]
        turned = jnp.transpose(jnp.concatenate([tile[:8] for tile in tiles], axis=0))
        for i, tile in enumerate(tiles):
            wide[i : i + 1, :] = tile[8:9]
        rows = dot(wide[:C, :].astype(BF16), pick)
        for half in range(2):
            lanes = pl.ds(pl.multiple_of(half * 512 + at * B, B), B)
            second_ref[:, lanes] = turned[half * 64 : (half + 1) * 64]
            for ref, q in ((gdecay_ref, half), (gskip_ref, 2 + half)):
                part = jnp.where(own, rows[:, q * B : (q + 1) * B], 0.0)
                ref[:, lanes] = jnp.sum(part, axis=0, keepdims=True)
        return carry

    lax.fori_loop(0, 4, columns, 0)

    wait_bytes(grad_in, SEQ - 1, cg_sem)

    def rows_kv(at, carry):
        for half in range(2):
            lanes = pl.ds(pl.multiple_of(half * 512 + at * B, B), B)
            grad = to_rows(grad_in, at, half)
            gk_ref[:, lanes] = (v_ref[:, lanes].astype(F32) * grad).astype(BF16)
            gv_ref[:, lanes] = (k_ref[:, lanes].astype(F32) * grad).astype(BF16)
        return carry

    lax.fori_loop(0, 4, rows_kv, 0)

    wait_bytes(fin, DEPTH - 1, f_sem)
    for i in range(DEPTH):
        wide[i : i + 1, :] = fin[i]
    total = wide[:C, :]
    first_ref[:16, :] = total[:, :64]
    first_ref[16:, :] = pltpu.roll(total, 64, 1)[:, :64]

    for at, ref in enumerate((send_x, send_g, back_x, back_g)):
        wait_bytes(ref, SEQ - 1, send_sem.at[at])
    wait_bytes(rs_out, DEPTH - 1, send_sem.at[4])
    wait_bytes(z_in, DEPTH - 1, send_sem.at[5])
    wait_bytes(plane_in, PLANE - 1, send_sem.at[6])
    wait_bytes(gather, PLANE - 1, send_sem.at[7])
    wait_bytes(tp_in, TP - 1, send_sem.at[8])
    wait_bytes(fin, DEPTH - 1, send_sem.at[9])


def copy_kernel(*refs):
    copies = [pltpu.make_async_copy(refs[i], refs[7 + i], refs[14].at[i]) for i in range(7)]
    for copy in copies:
        copy.start()
    for copy in copies:
        copy.wait()


def per_device(q_proj, k_proj, v_proj, grad_out, w_first, w_second, decay_rate, skip_gain):
    chan = decay_rate.shape[0]
    tables = [jnp.asarray(table) for table in make_tables()]
    rows = jax.ShapeDtypeStruct(q_proj.shape, BF16)
    block = pltpu.VMEM((J, C, B), BF16)
    full = pltpu.VMEM((J * C, B), F32)
    spectrum = pltpu.VMEM((C * J, 2 * B), F32)
    dma = pltpu.SemaphoreType.DMA
    anywhere = pl.BlockSpec(memory_space=pl.ANY)
    vmem = pl.BlockSpec(memory_space=pltpu.VMEM)
    operands = (
        q_proj, k_proj, v_proj, grad_out, w_first, w_second,
        decay_rate.reshape(1, chan), skip_gain.reshape(1, chan), *tables,
    )
    shapes = (
        rows,
        rows,
        rows,
        jax.ShapeDtypeStruct(w_first.shape, F32),
        jax.ShapeDtypeStruct(w_second.shape, F32),
        jax.ShapeDtypeStruct((1, chan), F32),
        jax.ShapeDtypeStruct((1, chan), F32),
    )
    results = pl.pallas_call(
        kernel,
        out_shape=[pltpu.VMEM(x.shape, x.dtype) for x in shapes],
        in_specs=[anywhere] * OPERANDS,
        out_specs=[vmem] * 7,
        scratch_shapes=[pltpu.VMEM(x.shape, x.dtype) for x in operands]
        + [block] * 8
        + [pltpu.VMEM((2, B, B), F32)]
        + [full] * 4
        + [pltpu.VMEM((J * 64, B), BF16)] * 2
        + [pltpu.VMEM((J * 64, B), F32)]
        + [spectrum] * 3
        + [pltpu.VMEM((B, B), F32)]
        + [pltpu.VMEM((DEPTH, C, B), BF16), pltpu.VMEM((PLANE, DEPTH, C, B), BF16)]
        + [pltpu.VMEM((count, 1, B), F32) for count in (DEPTH, DEPTH, PLANE, TP, DEPTH)]
        + [dma((10,))]
        + [dma(())] * 10
        + [dma((OPERANDS,))],
        compiler_params=pltpu.CompilerParams(
            collective_id=0, has_side_effects=True, vmem_limit_bytes=56 * 1024 * 1024
        ),
    )(*operands)
    results = [pltpu.with_memory_space_constraint(x, pltpu.VMEM) for x in results]
    grad_q, grad_k, grad_v, first, second, decay, skip = pl.pallas_call(
        copy_kernel,
        out_shape=shapes,
        in_specs=[vmem] * 7,
        out_specs=[anywhere] * 7,
        scratch_shapes=[dma((7,))],
    )(*results)
    return grad_q, grad_k, grad_v, first, second, decay.reshape(chan), skip.reshape(chan)


def solution(mesh):
    return jax.shard_map(
        per_device,
        mesh=mesh,
        in_specs=(
            P("seq", "tp"),
            P("seq", "tp"),
            P("seq", "tp"),
            P("seq", "tp"),
            P(),
            P(None, "tp"),
            P("tp"),
            P("tp"),
        ),
        out_specs=(
            P("seq", "tp"),
            P("seq", "tp"),
            P("seq", "tp"),
            P(),
            P(None, "tp"),
            P("tp"),
            P("tp"),
        ),
        check_vma=False,
    )
```

```python
import functools
import math

import jax
import jax.numpy as jnp
import numpy as np
from jax import lax
from jax.experimental import pallas as pl
from jax.experimental.pallas import tpu as pltpu
from jax.sharding import PartitionSpec as P

MESH = pl.DeviceIdType.MESH
F32 = jnp.float32
BF16 = jnp.bfloat16
J = 64
B = 128
C = 16
L = J * B
GROUP = 16
NET = 16
RED = 32
SEQ = 64
TP = 8
OPERANDS = 16
DEPTH = 16
PLANE = 4


def split_np(values):
    high = values.astype(np.float32).astype(jnp.bfloat16)
    low = (values - high.astype(np.float64)).astype(np.float32).astype(jnp.bfloat16)
    return high, low


def make_tables():
    turn = 2.0 * math.pi
    k1 = np.arange(J)[:, None] + 0.25
    first = turn * k1 * np.arange(J)[None, :] / J
    f1_high, f1_low = split_np(np.concatenate([np.cos(first), -np.sin(first)], axis=0))
    twiddle = turn * k1 * np.arange(B)[None, :] / L
    second = turn * (np.arange(B)[:, None] * np.arange(B)[None, :] % B) / B
    cos, sin = np.cos(second), np.sin(second)
    f2_high, f2_low = split_np(np.block([[cos, -sin], [sin, cos]]))
    i1_high, i1_low = split_np(np.block([[cos, sin], [-sin, cos]]))
    i2_high, i2_low = split_np(np.concatenate([np.cos(first.T), -np.sin(first.T)], axis=1) / L)
    band = np.arange(16)
    freq = 3 * (band + 1) ** 2 + band
    inner = turn * (freq[:, None] * np.arange(B)[None, :] % L) / L
    p_high, p_low = split_np(np.concatenate([np.sin(inner), np.cos(inner)], axis=0))
    outer = turn * (np.arange(J)[:, None] * freq[None, :] % J) / J
    pos_t = np.zeros((2 * B, B), np.float32).astype(jnp.bfloat16)
    pos_t[:B, :32], pos_t[:B, 32:64], pos_t[B:, :32] = p_high.T, p_low.T, p_high.T
    turn_cos = np.tile(np.concatenate([np.cos(outer), np.cos(outer)], axis=1), (1, 4))
    turn_sin = np.tile(np.concatenate([-np.sin(outer), np.sin(outer)], axis=1), (1, 4))
    return (
        np.concatenate([f1_high, f1_low], axis=1),
        np.concatenate([f1_high, f1_low, f1_high], axis=1),
        np.concatenate([f2_high, f2_high, f2_low], axis=0),
        np.concatenate([i1_high, i1_high, i1_low], axis=0),
        np.concatenate([i2_high, i2_low, i2_high], axis=1),
        np.concatenate([p_high, p_low, p_high, p_low], axis=0),
        pos_t,
        np.stack([np.cos(twiddle), np.sin(twiddle), turn_cos, turn_sin]).astype(np.float32),
    )


def dot(left, right):
    return jnp.dot(left, right, preferred_element_type=F32)


def split(values):
    high = values.astype(BF16)
    return high, (values - high.astype(F32)).astype(BF16)


def sin_cos(x):
    n = jnp.floor(x * (1.0 / math.pi) + 0.5)
    r = (x - n * 3.140625) - n * 9.6765358979e-4
    half = n * 0.5
    sign = 1.0 - 4.0 * (half - jnp.floor(half))
    s = r * r
    p = -1.0 / 39916800.0
    for factor in (1.0 / 362880.0, -1.0 / 5040.0, 1.0 / 120.0, -1.0 / 6.0):
        p = p * s + factor
    sine = (r + r * s * p) * sign
    q = 1.0 / 479001600.0
    for factor in (-1.0 / 3628800.0, 1.0 / 40320.0, -1.0 / 720.0, 1.0 / 24.0, -0.5, 1.0):
        q = q * s + factor
    return sine, q * sign


def kernel(*refs):
    inputs, outs, refs = refs[:OPERANDS], refs[OPERANDS : OPERANDS + 7], refs[OPERANDS + 7 :]
    held, refs = refs[:OPERANDS], refs[OPERANDS:]
    (
        q_ref, k_ref, v_ref, go_ref, w1_ref, w2_ref, decay_ref, skip_ref,
        f1x_ref, f1_ref, f2_ref, i1_ref, i2_ref, pb_ref, pt_ref, turns_ref,
    ) = held
    gq_ref, gk_ref, gv_ref, first_ref, second_ref, gdecay_ref, gskip_ref = outs
    (
        send_x, send_g, in_x, in_g, back_x, back_g, conv_in, grad_in,
        params, stage, stage_x, raw_ref, env_ref, hid_hi, hid_lo, cos_ref, spec_h, spec_x, spec_g, wide,
        z_in, gather, rs_out, rs_in, plane_in, tp_in, fin,
        send_sem, x_sem, g_sem, cx_sem, cg_sem, z_sem, rz_sem, y_sem, ry_sem, t_sem, f_sem, load_sem,
    ) = refs
    twc_ref, tws_ref, tc_ref, ts_ref = (turns_ref.at[i] for i in range(4))

    def load(at):
        return pltpu.make_async_copy(inputs[at], held[at], load_sem.at[at])

    load(1).start()
    load(2).start()

    me = lax.axis_index("seq")
    my_tp = lax.axis_index("tp")
    my_z, my_y = me // PLANE, me % PLANE
    scale = L**-0.5

    barrier = pltpu.get_barrier_semaphore()

    def greet(i, carry):
        pl.semaphore_signal(
            barrier, inc=1, device_id={"seq": (me + i) % SEQ}, device_id_type=MESH
        )
        return carry

    lax.fori_loop(1, SEQ, greet, 0)

    def greet_tp(i, carry):
        pl.semaphore_signal(
            barrier, inc=1, device_id={"tp": (my_tp + i) % TP}, device_id_type=MESH
        )
        return carry

    lax.fori_loop(1, TP, greet_tp, 0)

    for at in (0, *range(3, OPERANDS)):
        load(at).start()

    def gate(left_ref, right_ref, out_ref):
        def step(at, carry):
            parts = []
            for half in range(2):
                lanes = pl.ds(pl.multiple_of(half * 512 + at * B, B), B)
                gated = left_ref[:, lanes].astype(F32) * right_ref[:, lanes].astype(F32)
                parts.append(jnp.transpose(gated).reshape(16, 8, B))
            out_ref[pl.ds(at * 16, 16)] = jnp.concatenate(parts, axis=1).astype(BF16)
            return carry

        lax.fori_loop(0, 4, step, 0)

    def exchange(out_ref, in_ref, recv_sem, send_at, first, last):
        def send(peer):
            pltpu.make_async_remote_copy(
                src_ref=out_ref.at[peer],
                dst_ref=in_ref.at[me],
                send_sem=send_sem.at[send_at],
                recv_sem=recv_sem,
                device_id={"seq": peer},
                device_id_type=MESH,
            ).start()

        def step(i, carry):
            offset = (i * 11) % 32
            send((me + offset) % SEQ)
            send((me + SEQ - offset) % SEQ)
            return carry

        lax.fori_loop(max(first, 1), last, step, 0)
        if first == 0:
            send((me + SEQ // 2) % SEQ)
            in_ref[me] = out_ref[me]

    def wait_bytes(ref, count, sem):
        view = ref.at[pl.ds(0, count)]
        pltpu.make_async_copy(view, view, sem).wait()

    load(1).wait()
    load(2).wait()
    gate(k_ref, v_ref, send_x)
    pl.semaphore_wait(barrier, SEQ - 1 + TP - 1)
    exchange(send_x, in_x, x_sem, 0, 0, 32)
    load(0).wait()
    load(3).wait()
    gate(q_ref, go_ref, send_g)
    for at in range(4, OPERANDS):
        load(at).wait()

    for half in range(2):
        lanes = pl.ds(pl.multiple_of(half * 512 + (me // 16) * B, B), B)
        rows = lax.broadcasted_iota(jnp.int32, (64, B), 0)
        tail = jnp.where(
            rows == 0,
            jnp.broadcast_to(decay_ref[:, lanes], (64, B)),
            jnp.where(rows == 1, jnp.broadcast_to(skip_ref[:, lanes], (64, B)), 0.0),
        )
        params[half] = jnp.transpose(jnp.concatenate([w2_ref[:, lanes], tail], axis=0))
    pick = pl.ds(pl.multiple_of((me % 16) * 8, 8), 8)
    mine = jnp.concatenate([params[0, pick, :], params[1, pick, :]], axis=0)
    lane = lax.broadcasted_iota(jnp.int32, (C, B), 1)
    weights = jnp.where(lane < 64, mine, 0.0)
    decay = jnp.sum(jnp.where(lane == 64, mine, 0.0), axis=1, keepdims=True)
    skip = jnp.sum(jnp.where(lane == 65, mine, 0.0), axis=1, keepdims=True)
    w_high = weights.astype(BF16).astype(F32)
    w_low = (weights - w_high).astype(BF16).astype(F32)
    w_pair = w_high + pltpu.roll(w_low, 64, 1)
    w_rows = jnp.concatenate([w_pair, w_pair], axis=1).astype(BF16)
    wide[...] = jnp.zeros((B, B), F32)
    for at, part in enumerate((w_high, w_low, w_high, w_low)):
        wide[at * C : (at + 1) * C, :] = part
    w_cols = jnp.transpose(wide[...])[:64, :64].astype(BF16)

    w_one = w1_ref[...]
    w_swap = jnp.concatenate([w_one[16:], w_one[:16]], axis=0)
    wide[:, :64] = jnp.concatenate([w_one] * 4, axis=0)
    turned = jnp.transpose(wide[...])[:64]
    wide[:, :64] = jnp.concatenate([w_swap] * 4, axis=0)
    turned_swap = jnp.transpose(wide[...])[:64]
    lane_b = lax.broadcasted_iota(jnp.int32, (NET * 64, B), 1)
    position = lax.broadcasted_iota(jnp.int32, (C, B), 1).astype(F32)

    def network(at, carry):
        pieces = []
        for i in range(NET):
            j = at * NET + i
            pieces.append(turned * tc_ref[pl.ds(j, 1), :] + turned_swap * ts_ref[pl.ds(j, 1), :])
        values = jnp.concatenate(pieces, axis=0)
        high = values.astype(BF16).astype(F32)
        left = jnp.where(lane_b < 64, high, values - high).astype(BF16)
        sine, cosine = sin_cos(dot(left, pb_ref[...]))
        rows = pl.ds(pl.multiple_of(at * NET * 64, NET * 64), NET * 64)
        cos_ref[rows, :] = cosine
        high, low = split(sine)
        hid_hi[rows, :] = high
        hid_lo[rows, :] = low
        for i in range(0, NET, 2):
            h = jnp.concatenate([high[i * 64 : (i + 1) * 64], high[(i + 1) * 64 : (i + 2) * 64]], axis=1)
            l = jnp.concatenate([low[i * 64 : (i + 1) * 64], low[(i + 1) * 64 : (i + 2) * 64]], axis=1)
            raw = dot(w_rows, jnp.concatenate([h, h, l, l], axis=0))
            for o in range(2):
                j = at * NET + i + o
                fraction = (position + (j * B).astype(F32)) * (1.0 / L)
                envelope = jnp.exp(-decay * fraction) * scale
                part = raw[:, o * B : (o + 1) * B]
                here = pl.ds(pl.multiple_of(j * C, C), C)
                raw_ref[here, :] = part
                env_ref[here, :] = envelope
                stage[here, :] = part * envelope
        return carry

    lax.fori_loop(0, J // NET, network, 0)

    def forward(from_ref, spec_ref, exact):
        def step(at, carry):
            cols = [from_ref[pl.ds(at * GROUP + i, J, stride=C), :] for i in range(GROUP)]
            data = jnp.concatenate(cols, axis=1)
            if exact:
                data = data.astype(BF16)
                mixed = dot(f1x_ref[...], jnp.concatenate([data, data], axis=0))
            else:
                high, low = split(data)
                mixed = dot(f1_ref[...], jnp.concatenate([high, high, low], axis=0))
            turned = []
            for i in range(GROUP):
                re, im = mixed[:J, i * B : (i + 1) * B], mixed[J:, i * B : (i + 1) * B]
                c, s = twc_ref[...], tws_ref[...]
                turned.append(jnp.concatenate([re * c + im * s, im * c - re * s], axis=1))
            high, low = split(jnp.concatenate(turned, axis=0))
            rows = pl.ds(pl.multiple_of(at * GROUP * J, GROUP * J), GROUP * J)
            spec_ref[rows, :] = dot(jnp.concatenate([high, low, high], axis=1), f2_ref[...])
            return carry

        lax.fori_loop(0, C // GROUP, step, 0)

    def inverse(left_ref, right_ref, conjugate):
        def step(at, carry):
            rows = pl.ds(pl.multiple_of(at * GROUP * J, GROUP * J), GROUP * J)
            a, b = left_ref[rows, :], right_ref[rows, :]
            ar, ai, br, bi = a[:, :B], a[:, B:], b[:, :B], b[:, B:]
            if conjugate:
                product = jnp.concatenate([ar * br + ai * bi, ar * bi - ai * br], axis=1)
            else:
                product = jnp.concatenate([ar * br - ai * bi, ar * bi + ai * br], axis=1)
            high, low = split(product)
            mixed = dot(jnp.concatenate([high, low, high], axis=1), i1_ref[...])
            turned = []
            for i in range(GROUP):
                re, im = mixed[i * J : (i + 1) * J, :B], mixed[i * J : (i + 1) * J, B:]
                c, s = twc_ref[...], tws_ref[...]
                turned.append(jnp.concatenate([re * c - im * s, re * s + im * c], axis=0))
            high, low = split(jnp.concatenate(turned, axis=1))
            result = dot(i2_ref[...], jnp.concatenate([high, high, low], axis=0))
            for i in range(GROUP):
                stage[pl.ds(at * GROUP + i, J, stride=C), :] = result[:, i * B : (i + 1) * B]
            return carry

        lax.fori_loop(0, C // GROUP, step, 0)

    def finish(in_ref, out_ref):
        def step(at, carry):
            blocks = pl.ds(at * 8, 8)
            rows = pl.ds(pl.multiple_of(at * 8 * C, 8 * C), 8 * C)
            values = stage[rows, :].reshape(8, C, B) + skip[None] * in_ref[blocks].astype(F32)
            out_ref[blocks] = values.astype(BF16)
            return carry

        lax.fori_loop(0, J // 8, step, 0)

    def widen(in_ref, to_ref):
        def step(at, carry):
            rows = pl.ds(pl.multiple_of(at * 8 * C, 8 * C), 8 * C)
            to_ref[rows, :] = in_ref[pl.ds(at * 8, 8)].astype(F32).reshape(8 * C, B)
            return carry

        lax.fori_loop(0, J // 8, step, 0)

    forward(stage, spec_h, False)
    exchange(send_g, in_g, g_sem, 1, 0, 32)
    wait_bytes(in_x, SEQ - 1, x_sem)
    widen(in_x, stage_x)
    forward(stage_x, spec_x, True)
    inverse(spec_h, spec_x, False)
    finish(in_x, back_x)
    exchange(back_x, conv_in, cx_sem, 2, 0, 32)

    wait_bytes(in_g, SEQ - 1, g_sem)
    widen(in_g, stage)
    forward(stage, spec_g, True)
    inverse(spec_x, spec_g, True)

    def reduce_filter(at, carry):
        decay_sum, skip_sum, second, cos_sum, sin_sum = carry
        left, right, hid_rows = [], [], []
        for i in range(0, RED, 2):
            pair = []
            for j in (at * RED + i, at * RED + i + 1):
                here = pl.ds(pl.multiple_of(j * C, C), C)
                grad_raw = stage[here, :] * env_ref[here, :]
                fraction = (position + (j * B).astype(F32)) * (1.0 / L)
                decay_sum += grad_raw * raw_ref[here, :] * fraction
                skip_sum += in_x[j].astype(F32) * in_g[j].astype(F32)
                high, low = split(grad_raw)
                right.append(jnp.concatenate([high, low], axis=0))
                rows = pl.ds(pl.multiple_of(j * 64, 64), 64)
                hid_rows.append(jnp.concatenate([hid_hi[rows, :], hid_lo[rows, :]], axis=0))
                pair.append(jnp.concatenate([high, high, low, low], axis=0))
            both = dot(w_cols, jnp.concatenate(pair, axis=1))
            left += [both[:, :B], both[:, B:]]
        second += lax.dot_general(
            jnp.concatenate(hid_rows, axis=1),
            jnp.concatenate(right, axis=1),
            (((1,), (1,)), ((), ())),
            preferred_element_type=F32,
        )
        rows = pl.ds(pl.multiple_of(at * RED * 64, RED * 64), RED * 64)
        high, low = split(jnp.concatenate(left, axis=0) * cos_ref[rows, :])
        turned = dot(jnp.concatenate([high, low], axis=1), pt_ref[...])
        for i in range(RED):
            j = at * RED + i
            part = turned[i * 64 : (i + 1) * 64]
            cos_sum += part * tc_ref[pl.ds(j, 1), :]
            sin_sum += part * ts_ref[pl.ds(j, 1), :]
        return decay_sum, skip_sum, second, cos_sum, sin_sum

    zero = jnp.zeros((C, B), F32)
    decay_sum, skip_sum, second, cos_sum, sin_sum = lax.fori_loop(
        0,
        J // RED,
        reduce_filter,
        (zero, zero, jnp.zeros((B, 2 * C), F32), jnp.zeros((64, B), F32), jnp.zeros((64, B), F32)),
    )
    second = second[:64] + second[64:]
    wide[...] = jnp.zeros((B, B), F32)
    wide[:64, : 2 * C] = second * scale
    packed = jnp.transpose(wide[...])
    packed = packed[:C] + packed[C : 2 * C]
    packed = jnp.where(lane[:8] < 64, packed[:8], pltpu.roll(packed[8:], 64, 1))
    row = lax.broadcasted_iota(jnp.int32, (C, B), 0)
    sums = jnp.where(lane == row, -scale * jnp.sum(decay_sum, axis=1, keepdims=True), 0.0)
    sums += jnp.where(lane == row + C, scale * jnp.sum(skip_sum, axis=1, keepdims=True), 0.0)
    sums = jnp.sum(sums, axis=0, keepdims=True)

    cos_sum += pltpu.roll(cos_sum, B - 32, 1)
    sin_sum += pltpu.roll(sin_sum, B - 32, 1)
    lane_64 = lax.broadcasted_iota(jnp.int32, (64, B), 1)
    swapped = jnp.where(lane_64 < 16, pltpu.roll(sin_sum, B - 16, 1), pltpu.roll(sin_sum, 16, 1))
    wide[:64, :] = (cos_sum + swapped) * scale
    wide[64:, :] = jnp.zeros((64, B), F32)
    first = jnp.transpose(wide[...])
    first = jnp.where(lane < 64, first[:16], pltpu.roll(first[16:32], 64, 1))
    for i in range(DEPTH):
        rs_out[i] = first[i : i + 1]
    rs_in[my_z] = rs_out[my_z]
    wide[:8, :] = packed
    wide[8:9, :] = sums
    wide[9:16, :] = jnp.zeros((7, B), F32)
    z_in[my_z] = wide[:C, :].astype(BF16)

    def spread(ref, mine, sem, send_at, count, peer_of, parts=None):
        def step(i, carry):
            peer = (mine + i) % count
            pltpu.make_async_remote_copy(
                src_ref=ref.at[mine] if parts is None else parts.at[peer],
                dst_ref=ref.at[mine],
                send_sem=send_sem.at[send_at],
                recv_sem=sem,
                device_id=peer_of(peer),
                device_id_type=MESH,
            ).start()
            return carry

        lax.fori_loop(1, count, step, 0)

    def on_plane(peer):
        return {"seq": my_z * PLANE + peer}

    def on_depth(peer):
        return {"seq": peer * PLANE + my_y}

    spread(rs_in, my_z, rz_sem, 4, DEPTH, on_depth, rs_out)
    spread(z_in, my_z, z_sem, 5, DEPTH, on_depth)
    inverse(spec_h, spec_g, True)
    finish(in_g, back_g)
    exchange(back_g, grad_in, cg_sem, 3, 0, 32)

    def to_rows(in_ref, at, half):
        block = in_ref[pl.ds(at * 16, 16)].astype(F32)[:, half * 8 : (half + 1) * 8]
        return jnp.transpose(block.reshape(B, B))

    def add(ref, count):
        total = ref[0]
        for i in range(1, count):
            total += ref[i]
        return total

    wait_bytes(rs_in, DEPTH - 1, rz_sem)
    plane_in[my_y] = add(rs_in, DEPTH)
    spread(plane_in, my_y, ry_sem, 6, PLANE, on_plane)
    wait_bytes(z_in, DEPTH - 1, z_sem)
    gather[my_y] = z_in[...]
    spread(gather, my_y, y_sem, 7, PLANE, on_plane)
    wait_bytes(plane_in, PLANE - 1, ry_sem)
    tp_in[my_tp] = add(plane_in, PLANE)
    spread(tp_in, my_tp, t_sem, 8, TP, lambda peer: {"tp": peer})
    wait_bytes(conv_in, SEQ - 1, cx_sem)

    def rows_q(at, carry):
        for half in range(2):
            lanes = pl.ds(pl.multiple_of(half * 512 + at * B, B), B)
            gq_ref[:, lanes] = (go_ref[:, lanes].astype(F32) * to_rows(conv_in, at, half)).astype(BF16)
        return carry

    lax.fori_loop(0, 4, rows_q, 0, unroll=True)

    wait_bytes(tp_in, TP - 1, t_sem)
    fin[my_z] = add(tp_in, TP)
    spread(fin, my_z, f_sem, 9, DEPTH, on_depth)
    wait_bytes(gather, PLANE - 1, y_sem)

    source = lax.broadcasted_iota(jnp.int32, (B, 4 * B), 0)
    target = lax.broadcasted_iota(jnp.int32, (B, 4 * B), 1)
    pick = jnp.where(source == target // B * 8 + target % 8, 1.0, 0.0).astype(BF16)
    own = lane // 8 == lax.broadcasted_iota(jnp.int32, (C, B), 0)

    def columns(at, carry):
        tiles = [gather[y, at * 4 + z].astype(F32) for z in range(4) for y in range(PLANE)]
        turned = jnp.transpose(jnp.concatenate([tile[:8] for tile in tiles], axis=0))
        for i, tile in enumerate(tiles):
            wide[i : i + 1, :] = tile[8:9]
        rows = dot(wide[:C, :].astype(BF16), pick)
        for half in range(2):
            lanes = pl.ds(pl.multiple_of(half * 512 + at * B, B), B)
            second_ref[:, lanes] = turned[half * 64 : (half + 1) * 64]
            for ref, q in ((gdecay_ref, half), (gskip_ref, 2 + half)):
                part = jnp.where(own, rows[:, q * B : (q + 1) * B], 0.0)
                ref[:, lanes] = jnp.sum(part, axis=0, keepdims=True)
        return carry

    lax.fori_loop(0, 4, columns, 0)

    wait_bytes(grad_in, SEQ - 1, cg_sem)

    def rows_kv(at, carry):
        for half in range(2):
            lanes = pl.ds(pl.multiple_of(half * 512 + at * B, B), B)
            grad = to_rows(grad_in, at, half)
            gk_ref[:, lanes] = (v_ref[:, lanes].astype(F32) * grad).astype(BF16)
            gv_ref[:, lanes] = (k_ref[:, lanes].astype(F32) * grad).astype(BF16)
        return carry

    lax.fori_loop(0, 4, rows_kv, 0, unroll=True)

    wait_bytes(fin, DEPTH - 1, f_sem)
    for i in range(DEPTH):
        wide[i : i + 1, :] = fin[i]
    total = wide[:C, :]
    first_ref[:16, :] = total[:, :64]
    first_ref[16:, :] = pltpu.roll(total, 64, 1)[:, :64]

    for at, ref in enumerate((send_x, send_g, back_x, back_g)):
        wait_bytes(ref, SEQ - 1, send_sem.at[at])
    wait_bytes(rs_out, DEPTH - 1, send_sem.at[4])
    wait_bytes(z_in, DEPTH - 1, send_sem.at[5])
    wait_bytes(plane_in, PLANE - 1, send_sem.at[6])
    wait_bytes(gather, PLANE - 1, send_sem.at[7])
    wait_bytes(tp_in, TP - 1, send_sem.at[8])
    wait_bytes(fin, DEPTH - 1, send_sem.at[9])


def copy_kernel(*refs):
    copies = [pltpu.make_async_copy(refs[i], refs[7 + i], refs[14].at[i]) for i in range(7)]
    for copy in copies:
        copy.start()
    for copy in copies:
        copy.wait()


def per_device(q_proj, k_proj, v_proj, grad_out, w_first, w_second, decay_rate, skip_gain):
    chan = decay_rate.shape[0]
    tables = [jnp.asarray(table) for table in make_tables()]
    rows = jax.ShapeDtypeStruct(q_proj.shape, BF16)
    block = pltpu.VMEM((J, C, B), BF16)
    full = pltpu.VMEM((J * C, B), F32)
    spectrum = pltpu.VMEM((C * J, 2 * B), F32)
    dma = pltpu.SemaphoreType.DMA
    anywhere = pl.BlockSpec(memory_space=pl.ANY)
    vmem = pl.BlockSpec(memory_space=pltpu.VMEM)
    operands = (
        q_proj, k_proj, v_proj, grad_out, w_first, w_second,
        decay_rate.reshape(1, chan), skip_gain.reshape(1, chan), *tables,
    )
    shapes = (
        rows,
        rows,
        rows,
        jax.ShapeDtypeStruct(w_first.shape, F32),
        jax.ShapeDtypeStruct(w_second.shape, F32),
        jax.ShapeDtypeStruct((1, chan), F32),
        jax.ShapeDtypeStruct((1, chan), F32),
    )
    results = pl.pallas_call(
        kernel,
        out_shape=[pltpu.VMEM(x.shape, x.dtype) for x in shapes],
        in_specs=[anywhere] * OPERANDS,
        out_specs=[vmem] * 7,
        scratch_shapes=[pltpu.VMEM(x.shape, x.dtype) for x in operands]
        + [block] * 8
        + [pltpu.VMEM((2, B, B), F32)]
        + [full] * 4
        + [pltpu.VMEM((J * 64, B), BF16)] * 2
        + [pltpu.VMEM((J * 64, B), F32)]
        + [spectrum] * 3
        + [pltpu.VMEM((B, B), F32)]
        + [pltpu.VMEM((DEPTH, C, B), BF16), pltpu.VMEM((PLANE, DEPTH, C, B), BF16)]
        + [pltpu.VMEM((count, 1, B), F32) for count in (DEPTH, DEPTH, PLANE, TP, DEPTH)]
        + [dma((10,))]
        + [dma(())] * 10
        + [dma((OPERANDS,))],
        compiler_params=pltpu.CompilerParams(
            collective_id=0, has_side_effects=True, vmem_limit_bytes=56 * 1024 * 1024
        ),
    )(*operands)
    results = [pltpu.with_memory_space_constraint(x, pltpu.VMEM) for x in results]
    grad_q, grad_k, grad_v, first, second, decay, skip = pl.pallas_call(
        copy_kernel,
        out_shape=shapes,
        in_specs=[vmem] * 7,
        out_specs=[anywhere] * 7,
        scratch_shapes=[dma((7,))],
    )(*results)
    return grad_q, grad_k, grad_v, first, second, decay.reshape(chan), skip.reshape(chan)


def solution(mesh):
    return jax.shard_map(
        per_device,
        mesh=mesh,
        in_specs=(
            P("seq", "tp"),
            P("seq", "tp"),
            P("seq", "tp"),
            P("seq", "tp"),
            P(),
            P(None, "tp"),
            P("tp"),
            P("tp"),
        ),
        out_specs=(
            P("seq", "tp"),
            P("seq", "tp"),
            P("seq", "tp"),
            P(),
            P(None, "tp"),
            P("tp"),
            P("tp"),
        ),
        check_vma=False,
    )
```

```python
import functools
import math

import jax
import jax.numpy as jnp
import numpy as np
from jax import lax
from jax.experimental import pallas as pl
from jax.experimental.pallas import tpu as pltpu
from jax.sharding import PartitionSpec as P

MESH = pl.DeviceIdType.MESH
F32 = jnp.float32
BF16 = jnp.bfloat16
J = 64
B = 128
C = 16
L = J * B
GROUP = 16
NET = 16
RED = 32
SEQ = 64
TP = 8
OPERANDS = 16
DEPTH = 16
PLANE = 4


def split_np(values):
    high = values.astype(np.float32).astype(jnp.bfloat16)
    low = (values - high.astype(np.float64)).astype(np.float32).astype(jnp.bfloat16)
    return high, low


def make_tables():
    turn = 2.0 * math.pi
    k1 = np.arange(J)[:, None] + 0.25
    first = turn * k1 * np.arange(J)[None, :] / J
    f1_high, f1_low = split_np(np.concatenate([np.cos(first), -np.sin(first)], axis=0))
    twiddle = turn * k1 * np.arange(B)[None, :] / L
    second = turn * (np.arange(B)[:, None] * np.arange(B)[None, :] % B) / B
    cos, sin = np.cos(second), np.sin(second)
    f2_high, f2_low = split_np(np.block([[cos, -sin], [sin, cos]]))
    i1_high, i1_low = split_np(np.block([[cos, sin], [-sin, cos]]))
    i2_high, i2_low = split_np(np.concatenate([np.cos(first.T), -np.sin(first.T)], axis=1) / L)
    band = np.arange(16)
    freq = 3 * (band + 1) ** 2 + band
    inner = turn * (freq[:, None] * np.arange(B)[None, :] % L) / L
    p_high, p_low = split_np(np.concatenate([np.sin(inner), np.cos(inner)], axis=0))
    outer = turn * (np.arange(J)[:, None] * freq[None, :] % J) / J
    pos_t = np.zeros((2 * B, B), np.float32).astype(jnp.bfloat16)
    pos_t[:B, :32], pos_t[:B, 32:64], pos_t[B:, :32] = p_high.T, p_low.T, p_high.T
    turn_cos = np.tile(np.concatenate([np.cos(outer), np.cos(outer)], axis=1), (1, 4))
    turn_sin = np.tile(np.concatenate([-np.sin(outer), np.sin(outer)], axis=1), (1, 4))
    return (
        np.concatenate([f1_high, f1_low], axis=1),
        np.concatenate([f1_high, f1_low, f1_high], axis=1),
        np.concatenate([f2_high, f2_high, f2_low], axis=0),
        np.concatenate([i1_high, i1_high, i1_low], axis=0),
        np.concatenate([i2_high, i2_low, i2_high], axis=1),
        np.concatenate([p_high, p_low, p_high, p_low], axis=0),
        pos_t,
        np.stack([np.cos(twiddle), np.sin(twiddle), turn_cos, turn_sin]).astype(np.float32),
    )


def dot(left, right):
    return jnp.dot(left, right, preferred_element_type=F32)


def split(values):
    high = values.astype(BF16)
    return high, (values - high.astype(F32)).astype(BF16)


def sin_cos(x):
    n = jnp.floor(x * (1.0 / math.pi) + 0.5)
    r = (x - n * 3.140625) - n * 9.6765358979e-4
    half = n * 0.5
    sign = 1.0 - 4.0 * (half - jnp.floor(half))
    s = r * r
    p = -1.0 / 39916800.0
    for factor in (1.0 / 362880.0, -1.0 / 5040.0, 1.0 / 120.0, -1.0 / 6.0):
        p = p * s + factor
    sine = (r + r * s * p) * sign
    q = 1.0 / 479001600.0
    for factor in (-1.0 / 3628800.0, 1.0 / 40320.0, -1.0 / 720.0, 1.0 / 24.0, -0.5, 1.0):
        q = q * s + factor
    return sine, q * sign


def kernel(*refs):
    inputs, outs, refs = refs[:OPERANDS], refs[OPERANDS : OPERANDS + 7], refs[OPERANDS + 7 :]
    held, refs = refs[:OPERANDS], refs[OPERANDS:]
    (
        q_ref, k_ref, v_ref, go_ref, w1_ref, w2_ref, decay_ref, skip_ref,
        f1x_ref, f1_ref, f2_ref, i1_ref, i2_ref, pb_ref, pt_ref, turns_ref,
    ) = held
    gq_ref, gk_ref, gv_ref, first_ref, second_ref, gdecay_ref, gskip_ref = outs
    (
        send_x, send_g, in_x, in_g, back_x, back_g, conv_in, grad_in,
        params, stage, stage_x, raw_ref, env_ref, hid_hi, hid_lo, cos_ref, spec_h, spec_x, spec_g, wide,
        z_in, gather, rs_out, rs_in, plane_in, tp_in, fin,
        send_sem, x_sem, g_sem, cx_sem, cg_sem, z_sem, rz_sem, y_sem, ry_sem, t_sem, f_sem, load_sem,
    ) = refs
    twc_ref, tws_ref, tc_ref, ts_ref = (turns_ref.at[i] for i in range(4))

    def load(at):
        return pltpu.make_async_copy(inputs[at], held[at], load_sem.at[at])

    load(1).start()
    load(2).start()

    me = lax.axis_index("seq")
    my_tp = lax.axis_index("tp")
    my_z, my_y = me // PLANE, me % PLANE
    scale = L**-0.5

    barrier = pltpu.get_barrier_semaphore()

    def greet(i, carry):
        pl.semaphore_signal(
            barrier, inc=1, device_id={"seq": (me + i) % SEQ}, device_id_type=MESH
        )
        return carry

    lax.fori_loop(1, SEQ, greet, 0)

    def greet_tp(i, carry):
        pl.semaphore_signal(
            barrier, inc=1, device_id={"tp": (my_tp + i) % TP}, device_id_type=MESH
        )
        return carry

    lax.fori_loop(1, TP, greet_tp, 0)

    for at in (0, *range(3, OPERANDS)):
        load(at).start()

    def gate(left_ref, right_ref, out_ref):
        def step(at, carry):
            parts = []
            for half in range(2):
                lanes = pl.ds(pl.multiple_of(half * 512 + at * B, B), B)
                gated = left_ref[:, lanes].astype(F32) * right_ref[:, lanes].astype(F32)
                parts.append(jnp.transpose(gated).reshape(16, 8, B))
            out_ref[pl.ds(at * 16, 16)] = jnp.concatenate(parts, axis=1).astype(BF16)
            return carry

        lax.fori_loop(0, 4, step, 0, unroll=True)

    def exchange(out_ref, in_ref, recv_sem, send_at, first, last):
        def send(peer):
            pltpu.make_async_remote_copy(
                src_ref=out_ref.at[peer],
                dst_ref=in_ref.at[me],
                send_sem=send_sem.at[send_at],
                recv_sem=recv_sem,
                device_id={"seq": peer},
                device_id_type=MESH,
            ).start()

        def step(i, carry):
            offset = (i * 11) % 32
            send((me + offset) % SEQ)
            send((me + SEQ - offset) % SEQ)
            return carry

        lax.fori_loop(max(first, 1), last, step, 0)
        if first == 0:
            send((me + SEQ // 2) % SEQ)
            in_ref[me] = out_ref[me]

    def wait_bytes(ref, count, sem):
        view = ref.at[pl.ds(0, count)]
        pltpu.make_async_copy(view, view, sem).wait()

    load(1).wait()
    load(2).wait()
    gate(k_ref, v_ref, send_x)
    pl.semaphore_wait(barrier, SEQ - 1 + TP - 1)
    exchange(send_x, in_x, x_sem, 0, 0, 32)
    load(0).wait()
    load(3).wait()
    gate(q_ref, go_ref, send_g)
    for at in range(4, OPERANDS):
        load(at).wait()

    for half in range(2):
        lanes = pl.ds(pl.multiple_of(half * 512 + (me // 16) * B, B), B)
        rows = lax.broadcasted_iota(jnp.int32, (64, B), 0)
        tail = jnp.where(
            rows == 0,
            jnp.broadcast_to(decay_ref[:, lanes], (64, B)),
            jnp.where(rows == 1, jnp.broadcast_to(skip_ref[:, lanes], (64, B)), 0.0),
        )
        params[half] = jnp.transpose(jnp.concatenate([w2_ref[:, lanes], tail], axis=0))
    pick = pl.ds(pl.multiple_of((me % 16) * 8, 8), 8)
    mine = jnp.concatenate([params[0, pick, :], params[1, pick, :]], axis=0)
    lane = lax.broadcasted_iota(jnp.int32, (C, B), 1)
    weights = jnp.where(lane < 64, mine, 0.0)
    decay = jnp.sum(jnp.where(lane == 64, mine, 0.0), axis=1, keepdims=True)
    skip = jnp.sum(jnp.where(lane == 65, mine, 0.0), axis=1, keepdims=True)
    w_high = weights.astype(BF16).astype(F32)
    w_low = (weights - w_high).astype(BF16).astype(F32)
    w_pair = w_high + pltpu.roll(w_low, 64, 1)
    w_rows = jnp.concatenate([w_pair, w_pair], axis=1).astype(BF16)
    wide[...] = jnp.zeros((B, B), F32)
    for at, part in enumerate((w_high, w_low, w_high, w_low)):
        wide[at * C : (at + 1) * C, :] = part
    w_cols = jnp.transpose(wide[...])[:64, :64].astype(BF16)

    w_one = w1_ref[...]
    w_swap = jnp.concatenate([w_one[16:], w_one[:16]], axis=0)
    wide[:, :64] = jnp.concatenate([w_one] * 4, axis=0)
    turned = jnp.transpose(wide[...])[:64]
    wide[:, :64] = jnp.concatenate([w_swap] * 4, axis=0)
    turned_swap = jnp.transpose(wide[...])[:64]
    lane_b = lax.broadcasted_iota(jnp.int32, (NET * 64, B), 1)
    position = lax.broadcasted_iota(jnp.int32, (C, B), 1).astype(F32)

    def network(at, carry):
        pieces = []
        for i in range(NET):
            j = at * NET + i
            pieces.append(turned * tc_ref[pl.ds(j, 1), :] + turned_swap * ts_ref[pl.ds(j, 1), :])
        values = jnp.concatenate(pieces, axis=0)
        high = values.astype(BF16).astype(F32)
        left = jnp.where(lane_b < 64, high, values - high).astype(BF16)
        sine, cosine = sin_cos(dot(left, pb_ref[...]))
        rows = pl.ds(pl.multiple_of(at * NET * 64, NET * 64), NET * 64)
        cos_ref[rows, :] = cosine
        high, low = split(sine)
        hid_hi[rows, :] = high
        hid_lo[rows, :] = low
        for i in range(0, NET, 2):
            h = jnp.concatenate([high[i * 64 : (i + 1) * 64], high[(i + 1) * 64 : (i + 2) * 64]], axis=1)
            l = jnp.concatenate([low[i * 64 : (i + 1) * 64], low[(i + 1) * 64 : (i + 2) * 64]], axis=1)
            raw = dot(w_rows, jnp.concatenate([h, h, l, l], axis=0))
            for o in range(2):
                j = at * NET + i + o
                fraction = (position + (j * B).astype(F32)) * (1.0 / L)
                envelope = jnp.exp(-decay * fraction) * scale
                part = raw[:, o * B : (o + 1) * B]
                here = pl.ds(pl.multiple_of(j * C, C), C)
                raw_ref[here, :] = part
                env_ref[here, :] = envelope
                stage[here, :] = part * envelope
        return carry

    lax.fori_loop(0, J // NET, network, 0)

    def forward(from_ref, spec_ref, exact):
        def step(at, carry):
            cols = [from_ref[pl.ds(at * GROUP + i, J, stride=C), :] for i in range(GROUP)]
            data = jnp.concatenate(cols, axis=1)
            if exact:
                data = data.astype(BF16)
                mixed = dot(f1x_ref[...], jnp.concatenate([data, data], axis=0))
            else:
                high, low = split(data)
                mixed = dot(f1_ref[...], jnp.concatenate([high, high, low], axis=0))
            turned = []
            for i in range(GROUP):
                re, im = mixed[:J, i * B : (i + 1) * B], mixed[J:, i * B : (i + 1) * B]
                c, s = twc_ref[...], tws_ref[...]
                turned.append(jnp.concatenate([re * c + im * s, im * c - re * s], axis=1))
            high, low = split(jnp.concatenate(turned, axis=0))
            rows = pl.ds(pl.multiple_of(at * GROUP * J, GROUP * J), GROUP * J)
            spec_ref[rows, :] = dot(jnp.concatenate([high, low, high], axis=1), f2_ref[...])
            return carry

        lax.fori_loop(0, C // GROUP, step, 0)

    def inverse(left_ref, right_ref, conjugate):
        def step(at, carry):
            rows = pl.ds(pl.multiple_of(at * GROUP * J, GROUP * J), GROUP * J)
            a, b = left_ref[rows, :], right_ref[rows, :]
            ar, ai, br, bi = a[:, :B], a[:, B:], b[:, :B], b[:, B:]
            if conjugate:
                product = jnp.concatenate([ar * br + ai * bi, ar * bi - ai * br], axis=1)
            else:
                product = jnp.concatenate([ar * br - ai * bi, ar * bi + ai * br], axis=1)
            high, low = split(product)
            mixed = dot(jnp.concatenate([high, low, high], axis=1), i1_ref[...])
            turned = []
            for i in range(GROUP):
                re, im = mixed[i * J : (i + 1) * J, :B], mixed[i * J : (i + 1) * J, B:]
                c, s = twc_ref[...], tws_ref[...]
                turned.append(jnp.concatenate([re * c - im * s, re * s + im * c], axis=0))
            high, low = split(jnp.concatenate(turned, axis=1))
            result = dot(i2_ref[...], jnp.concatenate([high, high, low], axis=0))
            for i in range(GROUP):
                stage[pl.ds(at * GROUP + i, J, stride=C), :] = result[:, i * B : (i + 1) * B]
            return carry

        lax.fori_loop(0, C // GROUP, step, 0)

    def finish(in_ref, out_ref):
        def step(at, carry):
            blocks = pl.ds(at * 8, 8)
            rows = pl.ds(pl.multiple_of(at * 8 * C, 8 * C), 8 * C)
            values = stage[rows, :].reshape(8, C, B) + skip[None] * in_ref[blocks].astype(F32)
            out_ref[blocks] = values.astype(BF16)
            return carry

        lax.fori_loop(0, J // 8, step, 0)

    def widen(in_ref, to_ref):
        def step(at, carry):
            rows = pl.ds(pl.multiple_of(at * 8 * C, 8 * C), 8 * C)
            to_ref[rows, :] = in_ref[pl.ds(at * 8, 8)].astype(F32).reshape(8 * C, B)
            return carry

        lax.fori_loop(0, J // 8, step, 0)

    forward(stage, spec_h, False)
    exchange(send_g, in_g, g_sem, 1, 0, 32)
    wait_bytes(in_x, SEQ - 1, x_sem)
    widen(in_x, stage_x)
    forward(stage_x, spec_x, True)
    inverse(spec_h, spec_x, False)
    finish(in_x, back_x)
    exchange(back_x, conv_in, cx_sem, 2, 0, 32)

    wait_bytes(in_g, SEQ - 1, g_sem)
    widen(in_g, stage)
    forward(stage, spec_g, True)
    inverse(spec_x, spec_g, True)

    def reduce_filter(at, carry):
        decay_sum, skip_sum, second, cos_sum, sin_sum = carry
        left, right, hid_rows = [], [], []
        for i in range(0, RED, 2):
            pair = []
            for j in (at * RED + i, at * RED + i + 1):
                here = pl.ds(pl.multiple_of(j * C, C), C)
                grad_raw = stage[here, :] * env_ref[here, :]
                fraction = (position + (j * B).astype(F32)) * (1.0 / L)
                decay_sum += grad_raw * raw_ref[here, :] * fraction
                skip_sum += in_x[j].astype(F32) * in_g[j].astype(F32)
                high, low = split(grad_raw)
                right.append(jnp.concatenate([high, low], axis=0))
                rows = pl.ds(pl.multiple_of(j * 64, 64), 64)
                hid_rows.append(jnp.concatenate([hid_hi[rows, :], hid_lo[rows, :]], axis=0))
                pair.append(jnp.concatenate([high, high, low, low], axis=0))
            both = dot(w_cols, jnp.concatenate(pair, axis=1))
            left += [both[:, :B], both[:, B:]]
        second += lax.dot_general(
            jnp.concatenate(hid_rows, axis=1),
            jnp.concatenate(right, axis=1),
            (((1,), (1,)), ((), ())),
            preferred_element_type=F32,
        )
        rows = pl.ds(pl.multiple_of(at * RED * 64, RED * 64), RED * 64)
        high, low = split(jnp.concatenate(left, axis=0) * cos_ref[rows, :])
        turned = dot(jnp.concatenate([high, low], axis=1), pt_ref[...])
        for i in range(RED):
            j = at * RED + i
            part = turned[i * 64 : (i + 1) * 64]
            cos_sum += part * tc_ref[pl.ds(j, 1), :]
            sin_sum += part * ts_ref[pl.ds(j, 1), :]
        return decay_sum, skip_sum, second, cos_sum, sin_sum

    zero = jnp.zeros((C, B), F32)
    decay_sum, skip_sum, second, cos_sum, sin_sum = lax.fori_loop(
        0,
        J // RED,
        reduce_filter,
        (zero, zero, jnp.zeros((B, 2 * C), F32), jnp.zeros((64, B), F32), jnp.zeros((64, B), F32)),
    )
    second = second[:64] + second[64:]
    cos_sum += pltpu.roll(cos_sum, B - 32, 1)
    sin_sum += pltpu.roll(sin_sum, B - 32, 1)
    lane_64 = lax.broadcasted_iota(jnp.int32, (64, B), 1)
    swapped = jnp.where(lane_64 < 16, pltpu.roll(sin_sum, B - 16, 1), pltpu.roll(sin_sum, 16, 1))
    wide[:64, :] = (cos_sum + swapped) * scale
    wide[64:, :] = jnp.zeros((64, B), F32)
    first = jnp.transpose(wide[...])
    first = jnp.where(lane < 64, first[:16], pltpu.roll(first[16:32], 64, 1))
    for i in range(DEPTH):
        rs_out[i] = first[i : i + 1]
    rs_in[my_z] = rs_out[my_z]

    def spread(ref, mine, sem, send_at, count, peer_of, parts=None):
        def step(i, carry):
            peer = (mine + i) % count
            pltpu.make_async_remote_copy(
                src_ref=ref.at[mine] if parts is None else parts.at[peer],
                dst_ref=ref.at[mine],
                send_sem=send_sem.at[send_at],
                recv_sem=sem,
                device_id=peer_of(peer),
                device_id_type=MESH,
            ).start()
            return carry

        lax.fori_loop(1, count, step, 0)

    def on_plane(peer):
        return {"seq": my_z * PLANE + peer}

    def on_depth(peer):
        return {"seq": peer * PLANE + my_y}

    spread(rs_in, my_z, rz_sem, 4, DEPTH, on_depth, rs_out)
    wide[...] = jnp.zeros((B, B), F32)
    wide[:64, : 2 * C] = second * scale
    packed = jnp.transpose(wide[...])
    packed = packed[:C] + packed[C : 2 * C]
    packed = jnp.where(lane[:8] < 64, packed[:8], pltpu.roll(packed[8:], 64, 1))
    row = lax.broadcasted_iota(jnp.int32, (C, B), 0)
    sums = jnp.where(lane == row, -scale * jnp.sum(decay_sum, axis=1, keepdims=True), 0.0)
    sums += jnp.where(lane == row + C, scale * jnp.sum(skip_sum, axis=1, keepdims=True), 0.0)
    sums = jnp.sum(sums, axis=0, keepdims=True)
    wide[:8, :] = packed
    wide[8:9, :] = sums
    wide[9:16, :] = jnp.zeros((7, B), F32)
    z_in[my_z] = wide[:C, :].astype(BF16)
    spread(z_in, my_z, z_sem, 5, DEPTH, on_depth)
    inverse(spec_h, spec_g, True)
    finish(in_g, back_g)
    exchange(back_g, grad_in, cg_sem, 3, 0, 32)

    def to_rows(in_ref, at, half):
        block = in_ref[pl.ds(at * 16, 16)].astype(F32)[:, half * 8 : (half + 1) * 8]
        return jnp.transpose(block.reshape(B, B))

    def add(ref, count):
        total = ref[0]
        for i in range(1, count):
            total += ref[i]
        return total

    wait_bytes(rs_in, DEPTH - 1, rz_sem)
    plane_in[my_y] = add(rs_in, DEPTH)
    spread(plane_in, my_y, ry_sem, 6, PLANE, on_plane)
    wait_bytes(z_in, DEPTH - 1, z_sem)
    gather[my_y] = z_in[...]
    spread(gather, my_y, y_sem, 7, PLANE, on_plane)
    wait_bytes(plane_in, PLANE - 1, ry_sem)
    tp_in[my_tp] = add(plane_in, PLANE)
    spread(tp_in, my_tp, t_sem, 8, TP, lambda peer: {"tp": peer})
    wait_bytes(conv_in, SEQ - 1, cx_sem)

    def rows_q(at, carry):
        for half in range(2):
            lanes = pl.ds(pl.multiple_of(half * 512 + at * B, B), B)
            gq_ref[:, lanes] = (go_ref[:, lanes].astype(F32) * to_rows(conv_in, at, half)).astype(BF16)
        return carry

    lax.fori_loop(0, 4, rows_q, 0, unroll=True)

    wait_bytes(tp_in, TP - 1, t_sem)
    fin[my_z] = add(tp_in, TP)
    spread(fin, my_z, f_sem, 9, DEPTH, on_depth)
    wait_bytes(gather, PLANE - 1, y_sem)

    source = lax.broadcasted_iota(jnp.int32, (B, 4 * B), 0)
    target = lax.broadcasted_iota(jnp.int32, (B, 4 * B), 1)
    pick = jnp.where(source == target // B * 8 + target % 8, 1.0, 0.0).astype(BF16)
    own = lane // 8 == lax.broadcasted_iota(jnp.int32, (C, B), 0)

    def columns(at, carry):
        tiles = [gather[y, at * 4 + z].astype(F32) for z in range(4) for y in range(PLANE)]
        turned = jnp.transpose(jnp.concatenate([tile[:8] for tile in tiles], axis=0))
        for i, tile in enumerate(tiles):
            wide[i : i + 1, :] = tile[8:9]
        rows = dot(wide[:C, :].astype(BF16), pick)
        for half in range(2):
            lanes = pl.ds(pl.multiple_of(half * 512 + at * B, B), B)
            second_ref[:, lanes] = turned[half * 64 : (half + 1) * 64]
            for ref, q in ((gdecay_ref, half), (gskip_ref, 2 + half)):
                part = jnp.where(own, rows[:, q * B : (q + 1) * B], 0.0)
                ref[:, lanes] = jnp.sum(part, axis=0, keepdims=True)
        return carry

    lax.fori_loop(0, 4, columns, 0)

    wait_bytes(grad_in, SEQ - 1, cg_sem)

    def rows_kv(at, carry):
        for half in range(2):
            lanes = pl.ds(pl.multiple_of(half * 512 + at * B, B), B)
            grad = to_rows(grad_in, at, half)
            gk_ref[:, lanes] = (v_ref[:, lanes].astype(F32) * grad).astype(BF16)
            gv_ref[:, lanes] = (k_ref[:, lanes].astype(F32) * grad).astype(BF16)
        return carry

    lax.fori_loop(0, 4, rows_kv, 0, unroll=True)

    wait_bytes(fin, DEPTH - 1, f_sem)
    for i in range(DEPTH):
        wide[i : i + 1, :] = fin[i]
    total = wide[:C, :]
    first_ref[:16, :] = total[:, :64]
    first_ref[16:, :] = pltpu.roll(total, 64, 1)[:, :64]

    for at, ref in enumerate((send_x, send_g, back_x, back_g)):
        wait_bytes(ref, SEQ - 1, send_sem.at[at])
    wait_bytes(rs_out, DEPTH - 1, send_sem.at[4])
    wait_bytes(z_in, DEPTH - 1, send_sem.at[5])
    wait_bytes(plane_in, PLANE - 1, send_sem.at[6])
    wait_bytes(gather, PLANE - 1, send_sem.at[7])
    wait_bytes(tp_in, TP - 1, send_sem.at[8])
    wait_bytes(fin, DEPTH - 1, send_sem.at[9])


def copy_kernel(*refs):
    copies = [pltpu.make_async_copy(refs[i], refs[7 + i], refs[14].at[i]) for i in range(7)]
    for copy in copies:
        copy.start()
    for copy in copies:
        copy.wait()


def per_device(q_proj, k_proj, v_proj, grad_out, w_first, w_second, decay_rate, skip_gain):
    chan = decay_rate.shape[0]
    tables = [jnp.asarray(table) for table in make_tables()]
    rows = jax.ShapeDtypeStruct(q_proj.shape, BF16)
    block = pltpu.VMEM((J, C, B), BF16)
    full = pltpu.VMEM((J * C, B), F32)
    spectrum = pltpu.VMEM((C * J, 2 * B), F32)
    dma = pltpu.SemaphoreType.DMA
    anywhere = pl.BlockSpec(memory_space=pl.ANY)
    vmem = pl.BlockSpec(memory_space=pltpu.VMEM)
    operands = (
        q_proj, k_proj, v_proj, grad_out, w_first, w_second,
        decay_rate.reshape(1, chan), skip_gain.reshape(1, chan), *tables,
    )
    shapes = (
        rows,
        rows,
        rows,
        jax.ShapeDtypeStruct(w_first.shape, F32),
        jax.ShapeDtypeStruct(w_second.shape, F32),
        jax.ShapeDtypeStruct((1, chan), F32),
        jax.ShapeDtypeStruct((1, chan), F32),
    )
    results = pl.pallas_call(
        kernel,
        out_shape=[pltpu.VMEM(x.shape, x.dtype) for x in shapes],
        in_specs=[anywhere] * OPERANDS,
        out_specs=[vmem] * 7,
        scratch_shapes=[pltpu.VMEM(x.shape, x.dtype) for x in operands]
        + [block] * 8
        + [pltpu.VMEM((2, B, B), F32)]
        + [full] * 4
        + [pltpu.VMEM((J * 64, B), BF16)] * 2
        + [pltpu.VMEM((J * 64, B), F32)]
        + [spectrum] * 3
        + [pltpu.VMEM((B, B), F32)]
        + [pltpu.VMEM((DEPTH, C, B), BF16), pltpu.VMEM((PLANE, DEPTH, C, B), BF16)]
        + [pltpu.VMEM((count, 1, B), F32) for count in (DEPTH, DEPTH, PLANE, TP, DEPTH)]
        + [dma((10,))]
        + [dma(())] * 10
        + [dma((OPERANDS,))],
        compiler_params=pltpu.CompilerParams(
            collective_id=0, has_side_effects=True, vmem_limit_bytes=56 * 1024 * 1024
        ),
    )(*operands)
    results = [pltpu.with_memory_space_constraint(x, pltpu.VMEM) for x in results]
    grad_q, grad_k, grad_v, first, second, decay, skip = pl.pallas_call(
        copy_kernel,
        out_shape=shapes,
        in_specs=[vmem] * 7,
        out_specs=[anywhere] * 7,
        scratch_shapes=[dma((7,))],
    )(*results)
    return grad_q, grad_k, grad_v, first, second, decay.reshape(chan), skip.reshape(chan)


def solution(mesh):
    return jax.shard_map(
        per_device,
        mesh=mesh,
        in_specs=(
            P("seq", "tp"),
            P("seq", "tp"),
            P("seq", "tp"),
            P("seq", "tp"),
            P(),
            P(None, "tp"),
            P("tp"),
            P("tp"),
        ),
        out_specs=(
            P("seq", "tp"),
            P("seq", "tp"),
            P("seq", "tp"),
            P(),
            P(None, "tp"),
            P("tp"),
            P("tp"),
        ),
        check_vma=False,
    )
```
